32 devices in a mesh: leaf: 4 (over z), oct: 8 (over y, x, core).
Axes of the slice: x: 2, y: 2, z: 4, core: 2. Of those that a mesh axis runs over, the one named last changes fastest.
Arguments:
- fibre_solve: bfloat16 [384, 256, 256], P(('leaf', 'oct')), may hold values from -0.375 to 0.375
- fibre_rhs: bfloat16 [384, 256], P(('leaf', 'oct')), may hold values from -6 to 6
- fibre_points: float32 [384, 256], P(('leaf', 'oct')), may hold values from 0 to 1
- fibre_owner: int32 [384, 1], P(('leaf', 'oct')), may hold values from 0 to 7; in each aligned block of 12 rows (0 to 11, 12 to 23, ...) at most 3 rows name the same one
- shell_points: float32 [3, 128], P(None, ('leaf', 'oct')), may hold values from 0 to 1
- shell_block: bfloat16 [3, 128, 98304], P(None, ('leaf', 'oct')), may hold values from -0.01953125 to 0.01953125
- density: float32 [98304], P(('leaf', 'oct')), may hold values from -6 to 6
Outputs:
- fibre_flow: float32 [3, 24576], P(None, ('leaf', 'oct'))
- shell_flow: float32 [3, 128], P(None, ('leaf', 'oct'))
The draws below stay inside these ranges and needn't reach their ends.
Inputs may be any that keep to these rules, and one draw needn't show every extreme that they name: `fibre_owner`: among the 12 fibres of one device (an aligned block) no child box is named more than 3 times, and some child box is named exactly 3 times.
All inputs are finite; a program needn't handle non-finite values.
Results may differ from the reference program's by a relative error of at most 0.0012.
Values may be sent and summed in bfloat16 or wider, within the bound.
No kernel may reach another device: no remote copies, remote signals or barrier semaphores. Data moves between devices by JAX's collectives and lax.ppermute only.
A program may use at most 64 MiB of HBM per device.

```python
import math
import jax
import jax.numpy as jnp
import numpy as np
from jax import lax

NODES = 64
COLS = 98304
FIB_DEV = 12
SHP_DEV = 4
CAP = 3
FIBRES = 384
SHELL_PTS = 128
N_LEAF = 4
N_OCT = 8
DEVICES = 32


def levels(own_key, dims, shards, smallest, top_value):
    loudness, own = 1.0, jax.random.fold_in(own_key, 6)
    for axis_at, blocks in shards:
        draws = jnp.exp(jax.random.uniform(jax.random.fold_in(own, axis_at), (blocks,), jnp.float32, smallest / len(shards), top_value / len(shards)))
        loudness = loudness * jnp.repeat(draws, dims[axis_at] // blocks).reshape([-1 if axis == axis_at else 1 for axis in range(len(dims))])
    return loudness


def assign_block(rng, own, number, rows, count, top, reach, skew):
    order = jax.random.permutation(rng, count)
    crowded, ordinary = portions_of(count, rows * top, reach, skew, True), portions_of(count, rows * top, reach, skew, False)
    places = jnp.arange(count)

    def named(lengths, offset_by):
        used = int((lengths > 0).sum())
        fixed = max(1, used // 4)
        moved = fixed + (places - fixed + offset_by * (used - fixed)) % max(1, count - fixed)
        return jnp.zeros((count,), jnp.int32).at[order[jnp.where(places < fixed, places, moved)]].set(jnp.asarray(lengths, jnp.int32))

    lengths = jnp.where(number % 4 == 0, named(crowded, number // 4), named(ordinary, number - number // 4 - 1))
    mixed = jax.random.permutation(jax.random.fold_in(own, 3), count)
    giver, sink = mixed[0:count // 2 * 2:2], mixed[1:count // 2 * 2:2]
    margin = jnp.minimum(lengths[giver] - 1, reach - lengths[sink]) // 2
    margin = jnp.where((giver == order[0]) | (sink == order[0]) | (lengths[sink] == 0), 0, jnp.maximum(margin, 0))
    moved = jax.random.randint(jax.random.fold_in(own, 4), (count // 2,), 0, 1 << 20) % (margin + 1)
    lengths = lengths.at[giver].add(-moved).at[sink].add(moved)
    items = jnp.searchsorted(jnp.cumsum(lengths), jnp.arange(rows * top), side="right").astype(jnp.int32)
    listing = items.reshape(top, rows).T
    listing = listing[jax.random.permutation(jax.random.fold_in(own, 1), rows)]
    offset_by = jax.random.randint(jax.random.fold_in(own, 2), (rows, 1), 0, top)
    return jnp.take_along_axis(listing, (jnp.arange(top)[None, :] + offset_by) % top, axis=1)


def portions_of(amount, total, reach, slope, full):
    portions = [(1 << 20) // math.isqrt(grade ** slope) + 1 for grade in range(1, amount + 1)]
    largest = reach if full else min(reach, max(-(-total // amount), total * portions[0] // sum(portions)))
    least = 1 if total - largest >= amount - 1 else 0
    given, surplus = [largest] + [least] * (amount - 1), total - largest - least * (amount - 1)
    while surplus > 0:
        movable = [i for i in range(1, amount) if given[i] < largest] or [i for i in range(1, amount) if given[i] < reach]
        whole, remaining = sum([portions[i] for i in movable]), surplus
        for i in movable:
            more = min(reach - given[i], max(1, remaining * portions[i] // whole), surplus)
            given[i] = given[i] + more
            surplus = surplus - more
    return np.array(given)


def centred(own_key, dims, deviation, most, cuts=(), kind=jnp.bfloat16):
    gain = levels(own_key, dims, cuts, -0.22, 0.18) if cuts else 1.0
    drawn = jax.random.normal(own_key, dims, jnp.float32) * deviation * gain
    return jnp.minimum(jnp.maximum(drawn, -most), most).astype(kind)


def setup_inputs(seed: int = 0) -> dict:
    key_of = jax.random.split(jax.random.key(seed), 8)
    fibre_solve = centred(key_of[0], (FIBRES, 4 * NODES, 4 * NODES), (4 * NODES) ** -0.5, 0.375, ((0, 32),))
    fibre_rhs = centred(key_of[1], (FIBRES, 4 * NODES), 0.5, 6.0, ((0, 32),))
    fibre_points = jnp.clip(1.0 * jax.random.uniform(key_of[2], (FIBRES, 4 * NODES), jnp.float32) ** levels(key_of[2], (FIBRES, 4 * NODES), ((0, 32),), -0.2, 0.2), 0.0, 1.0)
    fibre_owner_keys = jax.random.split(jax.random.fold_in(key_of[3], 1), FIBRES // FIB_DEV)
    fibre_owner_turns = jax.random.permutation(jax.random.fold_in(key_of[3], 3), FIBRES // FIB_DEV)
    fibre_owner = jax.vmap(lambda own, number: assign_block(jax.random.fold_in(key_of[3], 2), own, number, FIB_DEV, N_OCT, 1, CAP, 2))(fibre_owner_keys, fibre_owner_turns).reshape((FIBRES, 1))
    shell_points = jnp.clip(1.0 * jax.random.uniform(key_of[4], (3, SHELL_PTS), jnp.float32) ** levels(key_of[4], (3, SHELL_PTS), ((1, 32),), -0.2, 0.2), 0.0, 1.0)
    shell_block = centred(key_of[5], (3, SHELL_PTS, COLS), COLS ** -0.5, 0.01953125, ((1, 32),))
    density = centred(key_of[6], (COLS,), 1.0, 6.0, ((0, 32),), jnp.float32)
    return {"fibre_solve": fibre_solve, "fibre_rhs": fibre_rhs, "fibre_points": fibre_points, "fibre_owner": fibre_owner, "shell_points": shell_points, "shell_block": shell_block, "density": density}


smooth_sq = 0.01
stokes_scale = 1.0 / (8.0 * math.pi)

def stokeslet(targets, sources):
    offset = targets[:, :, None] - sources[0:3, None, :]
    dist_sq = lax.optimization_barrier(jnp.sum(offset * offset, axis=0))
    shifted = dist_sq + smooth_sq
    weight = 1.0 / (shifted * jnp.sqrt(shifted))
    forces = sources[3:6]
    projected = lax.optimization_barrier(jnp.sum(offset * forces[:, None, :], axis=0)) + sources[6][None, :]
    direct = weight * (dist_sq + 2.0 * smooth_sq)
    stretch = jnp.einsum('ts,cs->ct', direct, forces, precision=lax.Precision.HIGHEST)
    pointing = lax.optimization_barrier(jnp.sum(offset * (weight * projected)[None], axis=2))
    return stokes_scale * (stretch + pointing)

def place_records(forces, points, owner_box, leaf_index):
    count_f = points.shape[0]
    node_count = points.shape[1] // 4
    local_xyz = points[:, :3 * node_count].reshape(count_f, 3, node_count)
    quad_weight = points[:, 3 * node_count:]
    corner = jnp.stack([2 * leaf_index + owner_box % 2, owner_box // 2 % 2, owner_box // 4], axis=1).astype(jnp.float32)
    position = local_xyz + corner[:, :, None]
    pushes = forces[:, :3 * node_count].reshape(count_f, 3, node_count) * quad_weight[:, None, :]
    source = forces[:, 3 * node_count:] * quad_weight
    return jnp.concatenate([position, pushes, source[:, None, :]], axis=1)

def box_centres(total_boxes):
    box_id = jnp.arange(total_boxes, dtype=jnp.int32)
    box_leaf = box_id // 8
    child_box = box_id % 8
    centres = jnp.stack([2 * box_leaf + child_box % 2, child_box // 2 % 2, child_box // 4]).astype(jnp.float32) + 0.5
    return (centres, box_leaf)

def reference(fibre_solve, fibre_rhs, fibre_points, fibre_owner, shell_points, shell_block, density):
    forces = jnp.einsum('fij,fj->fi', fibre_solve.astype(jnp.float32), fibre_rhs.astype(jnp.float32), precision=lax.Precision.HIGHEST)
    fibre_index = jnp.arange(FIBRES, dtype=jnp.int32)
    leaf_of = fibre_index // (FIB_DEV * N_OCT)
    owner_box = fibre_owner[:, 0]
    records = place_records(forces, fibre_points, owner_box, leaf_of)
    per_fibre = N_OCT * FIB_DEV
    per_box = records.reshape(N_LEAF, per_fibre, 7, NODES).transpose(0, 2, 1, 3).reshape(N_LEAF, 7, per_fibre * NODES)
    padded = jnp.pad(per_box, ((1, 1), (0, 0), (0, 0)))
    child_box = leaf_of * N_OCT + owner_box
    box_sums = lax.optimization_barrier(jnp.sum(records[:, 3:7], axis=2))
    onehot = (child_box[:, None] == jnp.arange(DEVICES, dtype=jnp.int32)[None, :]).astype(jnp.float32)
    moments = jnp.dot(onehot.T, box_sums, precision=lax.Precision.HIGHEST)
    centres, box_leaf = box_centres(DEVICES)
    shell_leaf = jnp.arange(SHELL_PTS, dtype=jnp.int32) // (SHP_DEV * N_OCT)
    shell_corner = jnp.stack([2 * shell_leaf, 0 * shell_leaf, 0 * shell_leaf]).astype(jnp.float32)
    abs_pos = 2.0 * shell_points + shell_corner
    shell_by_box = abs_pos.reshape(3, N_LEAF, N_OCT * SHP_DEV).transpose(1, 0, 2)

    def one_box(box_index):
        targets = jnp.concatenate([padded[box_index + 1][0:3], shell_by_box[box_index]], axis=1)
        running = jnp.zeros(targets.shape, jnp.float32)
        for neighbour in range(3):
            running = running + stokeslet(targets, padded[box_index + neighbour])
        far_mask = (jnp.abs(box_leaf - box_index) >= 2).astype(jnp.float32)
        far_sources = jnp.concatenate([centres, moments.T * far_mask[None, :]], axis=0)
        return running + stokeslet(targets, far_sources)
    flows = lax.map(one_box, jnp.arange(N_LEAF, dtype=jnp.int32))
    split_at = per_fibre * NODES
    fibre_flow = flows[:, :, :split_at].transpose(1, 0, 2).reshape(3, FIBRES * NODES)
    shell_near = flows[:, :, split_at:].transpose(1, 0, 2).reshape(3, SHELL_PTS)
    density_b = density.astype(jnp.bfloat16)
    shell_flow = jnp.einsum('cpk,k->cp', shell_block.astype(jnp.float32), density_b.astype(jnp.float32), precision=lax.Precision.HIGHEST) + shell_near
    return (fibre_flow, shell_flow)
```

```python
import functools
import math

import jax
import jax.numpy as jnp
from jax import lax
from jax.experimental import pallas as pl
from jax.experimental.pallas import tpu as pltpu
from jax.sharding import PartitionSpec as P

smooth_sq = 0.01
stokes_scale = 1.0 / (8.0 * math.pi)
F32 = jnp.float32
BF16 = jnp.bfloat16
VMEM = pl.BlockSpec(memory_space=pltpu.VMEM)
PARAMS = pltpu.CompilerParams(vmem_limit_bytes=40 * 2**20)


def split3(value):
    high = value.astype(BF16).astype(F32)
    rest = value - high
    middle = rest.astype(BF16).astype(F32)
    return high, middle, (rest - middle).astype(BF16).astype(F32)


def prepare_kernel(solve_ref, rhs_ref, points_ref, owner_ref, density_ref, record_ref, extra_ref):
    fibres, quads = rhs_ref.shape
    nodes = quads // 4
    width = record_ref.shape[1]
    rhs = rhs_ref[...]
    row = lax.broadcasted_iota(jnp.int32, (fibres, quads), 0)
    forces = jnp.zeros((fibres, quads), F32)
    for f in range(fibres):
        product = lax.dot_general(
            rhs, solve_ref[f], (((1,), (1,)), ((), ())), preferred_element_type=F32
        )
        forces = jnp.where(row == f, product, forces)
    points = points_ref[...]
    quad_weight = points[:, 3 * nodes :]
    pushes = forces * jnp.concatenate([quad_weight] * 4, axis=1)
    owner = owner_ref[...]
    corner = [owner % 2, owner // 2 % 2, owner // 4]
    place = [
        points[:, c * nodes : (c + 1) * nodes] + (corner[c].astype(F32) - 1.0) for c in range(3)
    ]
    record_ref[3:4, :] = jnp.zeros((1, width), F32)
    for f in range(fibres):
        lanes = slice(f * nodes, (f + 1) * nodes)
        for c in range(3):
            record_ref[c : c + 1, lanes] = place[c][f : f + 1, :]
        for c in range(4):
            record_ref[4 + c : 5 + c, lanes] = pushes[f : f + 1, c * nodes : (c + 1) * nodes]
    lane = lax.broadcasted_iota(jnp.int32, (fibres, width), 1)
    owned = lane == owner + 8 * lax.axis_index("leaf")
    for c in range(4):
        box_sum = jnp.sum(pushes[:, c * nodes : (c + 1) * nodes], axis=1, keepdims=True)
        extra_ref[c : c + 1, :] = jnp.sum(jnp.where(owned, box_sum, 0.0), axis=0, keepdims=True)
    rows = density_ref.shape[0]
    extra_ref[4 : 4 + rows, :] = density_ref[...].astype(BF16).astype(F32)


def prepare(fibre_solve, fibre_rhs, fibre_points, fibre_owner, density_rows):
    width = fibre_points.shape[0] * fibre_points.shape[1] // 4
    extra_rows = 4 + density_rows.shape[0]
    return pl.pallas_call(
        prepare_kernel,
        out_shape=(
            jax.ShapeDtypeStruct((8, width), F32),
            jax.ShapeDtypeStruct((extra_rows, width), F32),
        ),
        in_specs=[VMEM] * 5,
        out_specs=(VMEM, VMEM),
        compiler_params=PARAMS,
        name="prepare",
    )(fibre_solve, fibre_rhs, fibre_points, fibre_owner, density_rows)


def target_rows(place):
    sq = jnp.sum(place * place, axis=0, keepdims=True)
    high, middle, low = split3(place)
    one = jnp.ones_like(sq)
    zero = jnp.zeros_like(sq)
    sq_parts = split3(sq)
    return jnp.concatenate(
        [-2.0 * high, one] * 3
        + [-2.0 * middle, zero] * 2
        + [-2.0 * low, zero]
        + list(sq_parts)
        + [zero] * 5,
        axis=0,
    ).astype(BF16)


def source_rows(place):
    sq = jnp.sum(place * place, axis=0, keepdims=True) + smooth_sq
    high, middle, low = split3(jnp.concatenate([place, sq], axis=0))
    one = jnp.ones((3, place.shape[1]), F32)
    zero = jnp.zeros((5, place.shape[1]), F32)
    return jnp.concatenate([high, middle, low, high, middle, high, one, zero], axis=0).astype(BF16)


def source_terms(place, push, source):
    sq = jnp.sum(place * place, axis=0, keepdims=True) + 2.0 * smooth_sq
    rest = source - jnp.sum(place * push, axis=0, keepdims=True)
    terms = jnp.concatenate(
        [push, rest, sq * push - rest * place] + [place[a : a + 1] * push for a in range(3)], axis=0
    )
    return jnp.concatenate(split3(terms), axis=0).astype(BF16)


def add_sources(target_ref, rows, terms, total_ref, block):
    targets = target_ref.shape[1]
    width = rows.shape[1]
    step = min(block, width)
    for t in range(0, targets, block):
        total = None
        for s in range(0, width, step):
            d = lax.dot_general(
                rows[:, s : s + step],
                target_ref[:, t : t + block],
                (((0,), (0,)), ((), ())),
                preferred_element_type=F32,
            )
            inverse = lax.rsqrt(d)
            cube = inverse * inverse * inverse
            high = cube.astype(BF16)
            low = (cube - high.astype(F32)).astype(BF16)
            term = terms[:, s : s + step]
            part = jnp.dot(
                jnp.concatenate([term, term], axis=1),
                jnp.concatenate([high, low], axis=0),
                preferred_element_type=F32,
            )
            total = part if total is None else total + part
        total_ref[:, t : t + block] += total


def point_columns(points):
    count = points.shape[1]
    eye = lax.broadcasted_iota(jnp.int32, (count, count), 0) == lax.broadcasted_iota(
        jnp.int32, (count, count), 1
    )
    return [
        2.0 * jnp.sum(jnp.where(eye, points[c : c + 1], 0.0), axis=1, keepdims=True) - 1.0
        for c in range(3)
    ]


def direct(columns, place, push, source):
    offset = [columns[c] - place[c : c + 1] for c in range(3)]
    sq = offset[0] * offset[0] + offset[1] * offset[1] + offset[2] * offset[2]
    inverse = lax.rsqrt(sq + smooth_sq)
    cube = inverse * inverse * inverse
    along = source + (
        offset[0] * push[0:1] + offset[1] * push[1:2] + offset[2] * push[2:3]
    )
    spread = cube * (sq + 2.0 * smooth_sq)
    along = cube * along
    return [spread * push[c : c + 1] + along * offset[c] for c in range(3)]


def fold(value, lanes):
    total = value[:, :lanes]
    for at in range(lanes, value.shape[1], lanes):
        total = total + value[:, at : at + lanes]
    return total


def near_kernel(shift, first, *refs):
    if first:
        records_ref, own_ref, shell_ref, total_ref, shell_total_ref, target_ref, sum_ref = refs
    else:
        (records_ref, own_ref, shell_ref, total_in, shell_in) = refs[:5]
        total_ref, shell_total_ref, target_ref, sum_ref = refs[5:]
    target_ref[...] = target_rows(own_ref[0:3, :])
    sum_ref[...] = jnp.zeros_like(sum_ref)
    if first:
        shell_total_ref[...] = jnp.zeros_like(shell_total_ref)
    else:
        shell_total_ref[...] = shell_in[...]
    columns = point_columns(shell_ref[...])

    def body(j, carry):
        record = records_ref[j]
        place = record[0:3]
        if shift:
            axis = lax.broadcasted_iota(jnp.int32, place.shape, 0)
            place = place + jnp.where(axis == 0, float(shift), 0.0)
        push, source = record[4:7], record[7:8]
        add_sources(target_ref, source_rows(place), source_terms(place, push, source), sum_ref, 256)
        for c, value in enumerate(direct(columns, place, push, source)):
            shell_total_ref[c] += fold(value, 128)
        return carry

    lax.fori_loop(0, records_ref.shape[0], body, 0)
    terms = sum_ref.shape[0] // 3
    total = sum_ref[0:terms] + sum_ref[terms : 2 * terms] + sum_ref[2 * terms :]
    total_ref[...] = total if first else total + total_in[...]


def near(records, own, shell_points, shift, totals):
    targets = own.shape[1]
    count = shell_points.shape[1]
    out = (
        jax.ShapeDtypeStruct((16, targets), F32),
        jax.ShapeDtypeStruct((3, count, 128), F32),
    )
    pairs = records.shape[0] * records.shape[2] * targets
    return pl.pallas_call(
        functools.partial(near_kernel, shift, totals is None),
        out_shape=out,
        in_specs=[VMEM] * (3 if totals is None else 5),
        out_specs=(VMEM, VMEM),
        scratch_shapes=[pltpu.VMEM((32, targets), BF16), pltpu.VMEM((48, targets), F32)],
        compiler_params=PARAMS,
        cost_estimate=pl.CostEstimate(
            flops=500 * pairs, bytes_accessed=records.size * 4, transcendentals=pairs
        ),
        name="near",
    )(records, own, shell_points, *(totals or ()))


def finish_kernel(
    leaves,
    octants,
    own_ref,
    shell_ref,
    extras_ref,
    block_ref,
    total_in,
    shell_in,
    flow_ref,
    shell_flow_ref,
    target_ref,
    sum_ref,
):
    leaf, octant = lax.axis_index("leaf"), lax.axis_index("oct")
    width = extras_ref.shape[2]
    moments = jnp.zeros((4, width), F32)
    for at in range(leaves * octants):
        moments = moments + extras_ref[at, 0:4, :]
    boxes = -(-leaves * 8 // 128) * 128
    moments = moments[:, :boxes]
    box = lax.broadcasted_iota(jnp.int32, (1, boxes), 1)
    away = box // 8 - leaf
    far = (jnp.abs(away) >= 2) & (box < leaves * 8)
    child = box % 8
    place = jnp.concatenate(
        [
            (2 * away + child % 2).astype(F32) - 0.5,
            (child // 2 % 2).astype(F32) - 0.5,
            (child // 4).astype(F32) - 0.5,
        ],
        axis=0,
    )
    push = jnp.where(far, moments[0:3], 0.0)
    source = jnp.where(far, moments[3:4], 0.0)
    x = own_ref[0:3, :]
    target_ref[...] = target_rows(x)
    sum_ref[...] = jnp.zeros_like(sum_ref)
    add_sources(target_ref, source_rows(place), source_terms(place, push, source), sum_ref, 256)
    terms = sum_ref.shape[0] // 3
    total = total_in[...] + (
        sum_ref[0:terms] + sum_ref[terms : 2 * terms] + sum_ref[2 * terms :]
    )
    push_sum, rest_sum, constant = total[0:3], total[3:4], total[4:7]
    cross = [total[7 + 3 * a : 10 + 3 * a] for a in range(3)]
    flow = (
        jnp.sum(x * x, axis=0, keepdims=True) * push_sum
        + constant
        + x * (jnp.sum(x * push_sum, axis=0, keepdims=True) + rest_sum)
    )
    for a in range(3):
        flow = flow - 2.0 * x[a : a + 1] * cross[a]
    turned = [
        jnp.sum(x * cross[c], axis=0, keepdims=True) for c in range(3)
    ]
    flow_ref[...] = stokes_scale * (flow - jnp.concatenate(turned, axis=0))
    columns = point_columns(shell_ref[...])
    shell = [
        jnp.sum(shell_in[c] + fold(value, 128), axis=1, keepdims=True)
        for c, value in enumerate(direct(columns, place, push, source))
    ]
    rows = extras_ref.shape[1] - 4
    count = block_ref.shape[1]

    def body(at, sums):
        owner = ((at // octants) ^ leaf) * octants + ((at % octants) ^ octant)
        for r in range(rows):
            start = pl.multiple_of((owner * rows + r) * width, 128)
            dens = extras_ref[at, 4 + r : 5 + r, :]
            sums = tuple(
                sums[c] + block_ref[c, :, pl.ds(start, width)].astype(F32) * dens for c in range(3)
            )
        return sums

    zero = jnp.zeros((count, width), F32)
    sums = lax.fori_loop(0, leaves * octants, body, (zero, zero, zero))
    product = [jnp.sum(sums[c], axis=1, keepdims=True) for c in range(3)]
    eye = lax.broadcasted_iota(jnp.int32, (count, count), 0) == lax.broadcasted_iota(
        jnp.int32, (count, count), 1
    )
    for c in range(3):
        column = product[c] + stokes_scale * shell[c]
        shell_flow_ref[c : c + 1, :] = jnp.sum(jnp.where(eye, column, 0.0), axis=0, keepdims=True)


def finish(leaves, octants, own, shell_points, extras, shell_block, totals):
    targets = own.shape[1]
    return pl.pallas_call(
        functools.partial(finish_kernel, leaves, octants),
        out_shape=(
            jax.ShapeDtypeStruct((3, targets), F32),
            jax.ShapeDtypeStruct(shell_points.shape, F32),
        ),
        in_specs=[VMEM] * 6,
        out_specs=(VMEM, VMEM),
        scratch_shapes=[pltpu.VMEM((32, targets), BF16), pltpu.VMEM((48, targets), F32)],
        compiler_params=PARAMS,
        name="finish",
    )(own, shell_points, extras, shell_block, *totals)


def exchange(value, axis, bit):
    count = lax.axis_size(axis)
    return lax.ppermute(value, axis, [(i, i ^ bit) for i in range(count)])


def gather(value, axis, bits):
    for bit in bits:
        value = jnp.concatenate([value, exchange(value, axis, bit)], axis=0)
    return value


def shards(fibre_solve, fibre_rhs, fibre_points, fibre_owner, shell_points, shell_block, density):
    octants = lax.axis_size("oct")
    leaves = lax.axis_size("leaf")
    width = fibre_points.shape[0] * fibre_points.shape[1] // 4
    record, extra = prepare(
        fibre_solve, fibre_rhs, fibre_points, fibre_owner, density.reshape(-1, width)
    )
    octant_bits = [1 << b for b in range(octants.bit_length() - 1)]
    leaf_bits = [1 << b for b in range(leaves.bit_length() - 1)]
    records = gather(record[None], "oct", octant_bits)
    extras = gather(extra[None], "oct", octant_bits)
    from_left = lax.ppermute(records, "leaf", [(i, i + 1) for i in range(leaves - 1)])
    from_right = lax.ppermute(records, "leaf", [(i + 1, i) for i in range(leaves - 1)])
    extras = gather(extras, "leaf", leaf_bits)
    totals = near(records, record, shell_points, 0, None)
    totals = near(from_left, record, shell_points, -2, totals)
    totals = near(from_right, record, shell_points, 2, totals)
    return finish(leaves, octants, record, shell_points, extras, shell_block, totals)


def solution(mesh):
    placed = (
        P(("leaf", "oct"), None, None),
        P(("leaf", "oct"), None),
        P(("leaf", "oct"), None),
        P(("leaf", "oct"), None),
        P(None, ("leaf", "oct")),
        P(None, ("leaf", "oct"), None),
        P(("leaf", "oct")),
    )
    return jax.shard_map(
        shards,
        mesh=mesh,
        in_specs=placed,
        out_specs=(P(None, ("leaf", "oct")), P(None, ("leaf", "oct"))),
        check_vma=False,
    )
```

```python
import functools
import math

import jax
import jax.numpy as jnp
from jax import lax
from jax.experimental import pallas as pl
from jax.experimental.pallas import tpu as pltpu
from jax.sharding import PartitionSpec as P

smooth_sq = 0.01
stokes_scale = 1.0 / (8.0 * math.pi)
F32 = jnp.float32
BF16 = jnp.bfloat16
VMEM = pl.BlockSpec(memory_space=pltpu.VMEM)
WHOLE = pltpu.CompilerParams(vmem_limit_bytes=64 * 2**20 - 2**17)
PARAMS = pltpu.CompilerParams(vmem_limit_bytes=40 * 2**20)


def split3(value):
    high = value.astype(BF16).astype(F32)
    rest = value - high
    middle = rest.astype(BF16).astype(F32)
    return high, middle, (rest - middle).astype(BF16).astype(F32)


def prepare_kernel(
    solve_hbm,
    rhs_hbm,
    points_hbm,
    owner_hbm,
    density_hbm,
    record_ref,
    dens_ref,
    solve_ref,
    rhs_ref,
    points_ref,
    density_ref,
    owner_ref,
    solve_sem,
    sem,
):
    fibres, quads = rhs_ref.shape
    nodes = quads // 4
    width = record_ref.shape[1]
    copies = [
        pltpu.make_async_copy(owner_hbm, owner_ref, sem.at[0]),
        pltpu.make_async_copy(points_hbm, points_ref, sem.at[1]),
        pltpu.make_async_copy(rhs_hbm, rhs_ref, sem.at[2]),
        pltpu.make_async_copy(density_hbm, density_ref, sem.at[3]),
    ]
    solves = [
        pltpu.make_async_copy(solve_hbm.at[f], solve_ref.at[f], solve_sem.at[f])
        for f in range(fibres)
    ]
    for copy in copies + solves:
        copy.start()
    for copy in copies:
        copy.wait()
    rows = dens_ref.shape[0]
    dens_ref[...] = jnp.concatenate(
        [density_ref[r * width : (r + 1) * width].reshape(1, width) for r in range(rows)], axis=0
    ).astype(BF16)
    row = lax.broadcasted_iota(jnp.int32, (fibres, 1), 0)
    owner = jnp.zeros((fibres, 1), jnp.int32)
    for f in range(fibres):
        owner = jnp.where(row == f, owner_ref[f], owner)
    points = points_ref[...]
    corner = [owner % 2, owner // 2 % 2, owner // 4]
    place = [
        points[:, c * nodes : (c + 1) * nodes] + (corner[c].astype(F32) - 1.0) for c in range(3)
    ]
    for f in range(fibres):
        lanes = slice(f * nodes, (f + 1) * nodes)
        for c in range(3):
            record_ref[c : c + 1, lanes] = place[c][f : f + 1, :]
    quad_weight = points[:, 3 * nodes :]
    rhs = rhs_ref[...]
    forces = jnp.zeros((fibres, quads), F32)
    for f in range(fibres):
        solves[f].wait()
        product = lax.dot_general(
            rhs, solve_ref[f], (((1,), (1,)), ((), ())), preferred_element_type=F32
        )
        forces = jnp.where(row == f, product, forces)
    pushes = forces * jnp.concatenate([quad_weight] * 4, axis=1)
    for f in range(fibres):
        lanes = slice(f * nodes, (f + 1) * nodes)
        for c in range(4):
            record_ref[4 + c : 5 + c, lanes] = pushes[f : f + 1, c * nodes : (c + 1) * nodes]
    lane = lax.broadcasted_iota(jnp.int32, (fibres, width), 1)
    sums = jnp.zeros((fibres, width), F32)
    for c in range(4):
        box_sum = jnp.sum(pushes[:, c * nodes : (c + 1) * nodes], axis=1, keepdims=True)
        sums = jnp.where(lane == owner + 8 * c, box_sum, sums)
    record_ref[3:4, :] = jnp.sum(sums, axis=0, keepdims=True)


def prepare(fibre_solve, fibre_rhs, fibre_points, fibre_owner, density):
    fibres, quads = fibre_points.shape
    width = fibres * quads // 4
    hbm = pl.BlockSpec(memory_space=pltpu.HBM)
    return pl.pallas_call(
        prepare_kernel,
        out_shape=(
            jax.ShapeDtypeStruct((8, width), F32),
            jax.ShapeDtypeStruct((density.shape[0] // width, width), BF16),
        ),
        in_specs=[hbm] * 5,
        out_specs=(VMEM, VMEM),
        scratch_shapes=[
            pltpu.VMEM(fibre_solve.shape, BF16),
            pltpu.VMEM(fibre_rhs.shape, BF16),
            pltpu.VMEM(fibre_points.shape, F32),
            pltpu.VMEM(density.shape, F32),
            pltpu.SMEM((fibres,), jnp.int32),
            pltpu.SemaphoreType.DMA((fibres,)),
            pltpu.SemaphoreType.DMA((4,)),
        ],
        compiler_params=WHOLE,
        name="prepare",
    )(fibre_solve, fibre_rhs, fibre_points, fibre_owner.reshape(fibres), density)


def target_rows(place):
    sq = jnp.sum(place * place, axis=0, keepdims=True)
    high, middle, low = split3(place)
    one = jnp.ones_like(sq)
    zero = jnp.zeros_like(sq)
    sq_parts = split3(sq)
    return jnp.concatenate(
        [-2.0 * high, one] * 3
        + [-2.0 * middle, zero] * 2
        + [-2.0 * low, zero]
        + list(sq_parts)
        + [zero] * 5,
        axis=0,
    ).astype(BF16)


def source_rows(place):
    sq = jnp.sum(place * place, axis=0, keepdims=True) + smooth_sq
    high, middle, low = split3(jnp.concatenate([place, sq], axis=0))
    one = jnp.ones((3, place.shape[1]), F32)
    zero = jnp.zeros((5, place.shape[1]), F32)
    return jnp.concatenate([high, middle, low, high, middle, high, one, zero], axis=0).astype(BF16)


def source_terms(place, push, source):
    sq = jnp.sum(place * place, axis=0, keepdims=True) + 2.0 * smooth_sq
    rest = source - jnp.sum(place * push, axis=0, keepdims=True)
    terms = jnp.concatenate(
        [push, rest, sq * push - rest * place] + [place[a : a + 1] * push for a in range(3)], axis=0
    )
    return jnp.concatenate(split3(terms), axis=0).astype(BF16)


def add_sources(target_ref, groups, total_ref, block):
    targets = target_ref.shape[1]
    lead = total_ref.shape[0] // 3
    totals = {}
    for rows, terms in groups:
        width = rows.shape[1]
        step = min(block, width)
        for t in range(0, targets, block):
            for s in range(0, width, step):
                d = lax.dot_general(
                    rows[:, s : s + step],
                    target_ref[:, t : t + block],
                    (((0,), (0,)), ((), ())),
                    preferred_element_type=F32,
                )
                inverse = lax.rsqrt(d)
                cube = inverse * inverse * inverse
                high = cube.astype(BF16)
                low = (cube - high.astype(F32)).astype(BF16)
                term = terms[:, s : s + step]
                part = jnp.dot(term, high, preferred_element_type=F32)
                rest = jnp.dot(term[:lead], low, preferred_element_type=F32)
                part = jnp.concatenate([part[:lead] + rest, part[lead:]], axis=0)
                totals[t] = totals[t] + part if t in totals else part
    for t, value in totals.items():
        total_ref[:, t : t + block] += value


def point_columns(points):
    count = points.shape[1]
    eye = lax.broadcasted_iota(jnp.int32, (count, count), 0) == lax.broadcasted_iota(
        jnp.int32, (count, count), 1
    )
    return [
        2.0 * jnp.sum(jnp.where(eye, points[c : c + 1], 0.0), axis=1, keepdims=True) - 1.0
        for c in range(3)
    ]


def direct(columns, place, push, source):
    offset = [columns[c] - place[c : c + 1] for c in range(3)]
    sq = offset[0] * offset[0] + offset[1] * offset[1] + offset[2] * offset[2]
    inverse = lax.rsqrt(sq + smooth_sq)
    cube = inverse * inverse * inverse
    along = source + (
        offset[0] * push[0:1] + offset[1] * push[1:2] + offset[2] * push[2:3]
    )
    spread = cube * (sq + 2.0 * smooth_sq)
    along = cube * along
    return [spread * push[c : c + 1] + along * offset[c] for c in range(3)]


def fold(value, lanes):
    total = value[:, :lanes]
    for at in range(lanes, value.shape[1], lanes):
        total = total + value[:, at : at + lanes]
    return total


def near_kernel(shift, first, *refs):
    if first:
        records_ref, own_ref, shell_ref, total_ref, shell_total_ref, target_ref, sum_ref = refs
    else:
        (records_ref, own_ref, shell_ref, total_in, shell_in) = refs[:5]
        total_ref, shell_total_ref, target_ref, sum_ref = refs[5:]
    target_ref[...] = target_rows(own_ref[0:3, :])
    sum_ref[...] = jnp.zeros_like(sum_ref)
    if first:
        shell_total_ref[...] = jnp.zeros_like(shell_total_ref)
    else:
        shell_total_ref[...] = shell_in[...]
    columns = point_columns(shell_ref[...])
    if shift is not None:
        moved = (2 * shift(lax.axis_index("leaf"))).astype(F32)
    count = records_ref.shape[0]
    unroll = max(u for u in range(1, 5) if count % u == 0)

    def body(at, carry):
        groups = []
        for j in range(unroll):
            record = records_ref[at * unroll + j]
            place = record[0:3]
            if shift is not None:
                axis = lax.broadcasted_iota(jnp.int32, place.shape, 0)
                place = place + jnp.where(axis == 0, moved, 0.0)
            push, source = record[4:7], record[7:8]
            groups.append((source_rows(place), source_terms(place, push, source)))
            for c, value in enumerate(direct(columns, place, push, source)):
                shell_total_ref[c] += fold(value, 128)
        add_sources(target_ref, groups, sum_ref, 256)
        return carry

    if count == unroll:
        body(0, 0)
    else:
        lax.fori_loop(0, count // unroll, body, 0)
    terms = sum_ref.shape[0] // 3
    total = sum_ref[0:terms] + sum_ref[terms : 2 * terms] + sum_ref[2 * terms :]
    total_ref[...] = total if first else total + total_in[...]


def near(records, own, shell_points, shift, totals):
    targets = own.shape[1]
    count = shell_points.shape[1]
    out = (
        jax.ShapeDtypeStruct((16, targets), F32),
        jax.ShapeDtypeStruct((3, count, 128), F32),
    )
    pairs = records.shape[0] * records.shape[2] * targets
    return pl.pallas_call(
        functools.partial(near_kernel, shift, totals is None),
        out_shape=out,
        in_specs=[VMEM] * (3 if totals is None else 5),
        out_specs=(VMEM, VMEM),
        scratch_shapes=[pltpu.VMEM((32, targets), BF16), pltpu.VMEM((48, targets), F32)],
        compiler_params=PARAMS,
        cost_estimate=pl.CostEstimate(
            flops=500 * pairs, bytes_accessed=records.size * 4, transcendentals=pairs
        ),
        name="near",
    )(records, own, shell_points, *(totals or ()))


def finish_kernel(
    order,
    own_ref,
    shell_ref,
    moments_ref,
    dens_ref,
    block_ref,
    total_in,
    shell_in,
    flow_ref,
    shell_flow_ref,
    target_ref,
    sum_ref,
):
    leaf, octant = lax.axis_index("leaf"), lax.axis_index("oct")
    leaves, octants = moments_ref.shape[0], len(order)
    boxes = -(-leaves * octants // 128) * 128
    moments = []
    for c in range(4):
        parts = [
            moments_ref[j][:, c * octants : (c + 1) * octants] for j in range(leaves)
        ]
        if boxes > leaves * octants:
            parts.append(jnp.zeros((1, boxes - leaves * octants), F32))
        moments.append(jnp.concatenate(parts, axis=1))
    box = lax.broadcasted_iota(jnp.int32, (1, boxes), 1)
    away = jnp.bitwise_xor(box // 8, leaf) - leaf
    far = (jnp.abs(away) >= 2) & (box < leaves * octants)
    away = jnp.where(far, away, 0)
    child = box % 8
    place = jnp.concatenate(
        [
            (2 * away + child % 2).astype(F32) - 0.5,
            (child // 2 % 2).astype(F32) - 0.5,
            (child // 4).astype(F32) - 0.5,
        ],
        axis=0,
    )
    push = jnp.where(far, jnp.concatenate(moments[0:3], axis=0), 0.0)
    source = jnp.where(far, moments[3], 0.0)
    x = own_ref[0:3, :]
    target_ref[...] = target_rows(x)
    sum_ref[...] = jnp.zeros_like(sum_ref)
    groups = [(source_rows(place), source_terms(place, push, source))]
    add_sources(target_ref, groups, sum_ref, 256)
    terms = sum_ref.shape[0] // 3
    total = total_in[...] + (
        sum_ref[0:terms] + sum_ref[terms : 2 * terms] + sum_ref[2 * terms :]
    )
    push_sum, rest_sum, constant = total[0:3], total[3:4], total[4:7]
    cross = [total[7 + 3 * a : 10 + 3 * a] for a in range(3)]
    flow = (
        jnp.sum(x * x, axis=0, keepdims=True) * push_sum
        + constant
        + x * (jnp.sum(x * push_sum, axis=0, keepdims=True) + rest_sum)
    )
    for a in range(3):
        flow = flow - 2.0 * x[a : a + 1] * cross[a]
    turned = [
        jnp.sum(x * cross[c], axis=0, keepdims=True) for c in range(3)
    ]
    flow_ref[...] = stokes_scale * (flow - jnp.concatenate(turned, axis=0))
    columns = point_columns(shell_ref[...])
    shell = [
        jnp.sum(shell_in[c] + fold(value, 128), axis=1, keepdims=True)
        for c, value in enumerate(direct(columns, place, push, source))
    ]
    rows, width = dens_ref.shape[1:]
    count = block_ref.shape[1]

    def body(at, sums):
        for j in range(octants):
            dens = dens_ref[at * octants + j].astype(F32)
            owner = jnp.bitwise_xor(at, leaf) * octants + jnp.bitwise_xor(octant, order[j])
            for r in range(rows):
                start = pl.multiple_of((owner * rows + r) * width, 128)
                sums = tuple(
                    sums[c] + block_ref[c, :, pl.ds(start, width)].astype(F32) * dens[r : r + 1]
                    for c in range(3)
                )
        return sums

    zero = jnp.zeros((count, width), F32)
    sums = lax.fori_loop(0, leaves, body, (zero, zero, zero))
    product = [jnp.sum(sums[c], axis=1, keepdims=True) for c in range(3)]
    eye = lax.broadcasted_iota(jnp.int32, (count, count), 0) == lax.broadcasted_iota(
        jnp.int32, (count, count), 1
    )
    for c in range(3):
        column = product[c] + stokes_scale * shell[c]
        shell_flow_ref[c : c + 1, :] = jnp.sum(jnp.where(eye, column, 0.0), axis=0, keepdims=True)


def finish(order, own, shell_points, moments, dens, shell_block, totals):
    targets = own.shape[1]
    return pl.pallas_call(
        functools.partial(finish_kernel, order),
        out_shape=(
            jax.ShapeDtypeStruct((3, targets), F32),
            jax.ShapeDtypeStruct(shell_points.shape, F32),
        ),
        in_specs=[VMEM] * 7,
        out_specs=(VMEM, VMEM),
        scratch_shapes=[pltpu.VMEM((32, targets), BF16), pltpu.VMEM((48, targets), F32)],
        compiler_params=PARAMS,
        name="finish",
    )(own, shell_points, moments, dens, shell_block, *totals)


def exchange(value, axis, bit):
    count = lax.axis_size(axis)
    return lax.ppermute(value, axis, [(i, i ^ bit) for i in range(count)])


def together(*values):
    return lax.optimization_barrier(values)


def shards(fibre_solve, fibre_rhs, fibre_points, fibre_owner, shell_points, shell_block, density):
    octants = lax.axis_size("oct")
    leaves = lax.axis_size("leaf")
    record, dens = prepare(fibre_solve, fibre_rhs, fibre_points, fibre_owner, density)
    bits = [1 << b for b in range(octants.bit_length() - 1)]
    bits = bits[1:] + bits[:1]
    order = [0]
    records, dens = record[None], dens[None]
    fresh, totals = records, None
    for bit in bits:
        arrived, arrived_dens = exchange(records, "oct", bit), exchange(dens, "oct", bit)
        order = order + [j ^ bit for j in order]
        if bit != bits[-1]:
            totals = near(fresh, record, shell_points, None, totals)
            arrived, arrived_dens, totals = together(arrived, arrived_dens, totals)
            fresh = arrived
        else:
            fresh = jnp.concatenate([fresh, arrived], axis=0)
        records = jnp.concatenate([records, arrived], axis=0)
        dens = jnp.concatenate([dens, arrived_dens], axis=0)
    moments = jnp.sum(records[:, 3, :128], axis=0)[None, None]
    half = fresh.shape[0] // 2
    inner = exchange(records, "leaf", 1)
    inner_dens, inner_moments = exchange(dens, "leaf", 1), exchange(moments, "leaf", 1)
    totals = near(fresh[:half], record, shell_points, None, totals)
    late, totals = together(records, totals)
    pairs = [(i, i + 1) for i in range(1, leaves - 1, 2)]
    outer = lax.ppermute(late, "leaf", pairs + [(j, i) for i, j in pairs])
    totals = near(fresh[half:], record, shell_points, None, totals)
    inner, inner_dens, inner_moments, totals = together(inner, inner_dens, inner_moments, totals)
    dens = jnp.concatenate([dens, inner_dens], axis=0)
    moments = jnp.concatenate([moments, inner_moments], axis=0)
    for bit in [1 << b for b in range(1, leaves.bit_length() - 1)]:
        dens = jnp.concatenate([dens, exchange(dens, "leaf", bit)], axis=0)
        moments = jnp.concatenate([moments, exchange(moments, "leaf", bit)], axis=0)
    totals = near(inner, record, shell_points, lambda leaf: 1 - 2 * (leaf % 2), totals)
    totals = near(outer, record, shell_points, lambda leaf: 2 * (leaf % 2) - 1, totals)
    return finish(tuple(order), record, shell_points, moments, dens, shell_block, totals)


def solution(mesh):
    placed = (
        P(("leaf", "oct"), None, None),
        P(("leaf", "oct"), None),
        P(("leaf", "oct"), None),
        P(("leaf", "oct"), None),
        P(None, ("leaf", "oct")),
        P(None, ("leaf", "oct"), None),
        P(("leaf", "oct")),
    )
    return jax.shard_map(
        shards,
        mesh=mesh,
        in_specs=placed,
        out_specs=(P(None, ("leaf", "oct")), P(None, ("leaf", "oct"))),
        check_vma=False,
    )
```

```python
import functools
import math

import jax
import jax.numpy as jnp
from jax import lax
from jax.experimental import pallas as pl
from jax.experimental.pallas import tpu as pltpu
from jax.sharding import PartitionSpec as P

smooth_sq = 0.01
stokes_scale = 1.0 / (8.0 * math.pi)
F32 = jnp.float32
BF16 = jnp.bfloat16
VMEM = pl.BlockSpec(memory_space=pltpu.VMEM)
PARAMS = pltpu.CompilerParams(vmem_limit_bytes=40 * 2**20)


def split3(value):
    high = value.astype(BF16).astype(F32)
    rest = value - high
    middle = rest.astype(BF16).astype(F32)
    return high, middle, (rest - middle).astype(BF16).astype(F32)


def prepare_kernel(*refs):
    solve_hbm, rhs_hbm, points_hbm, owner_hbm, density_hbm, shell_hbm = refs[:6]
    record_ref, shell_out = refs[6:8]
    solve_ref, rhs_ref, points_ref, density_ref, shell_ref, owner_ref, solve_sem, sem = refs[8:]
    fibres, quads = rhs_ref.shape
    nodes = quads // 4
    width = record_ref.shape[2]
    part = math.gcd(fibres, 4)
    copies = [
        pltpu.make_async_copy(owner_hbm, owner_ref, sem.at[0]),
        pltpu.make_async_copy(points_hbm, points_ref, sem.at[1]),
        pltpu.make_async_copy(rhs_hbm, rhs_ref, sem.at[2]),
        pltpu.make_async_copy(density_hbm, density_ref, sem.at[3]),
        pltpu.make_async_copy(shell_hbm, shell_ref, sem.at[4]),
    ]
    solves = [
        pltpu.make_async_copy(
            solve_hbm.at[pl.ds(f, part)], solve_ref.at[pl.ds(f, part)], solve_sem.at[f // part]
        )
        for f in range(0, fibres, part)
    ]
    for copy in copies + solves:
        copy.start()
    for copy in copies:
        copy.wait()
    shell_out[...] = shell_ref[...]
    record_ref[2] = jnp.zeros(record_ref.shape[1:], F32)
    for r in range(density_ref.shape[0] // width):
        dens = density_ref[r * width : (r + 1) * width].reshape(1, width)
        record_ref[2, r : r + 1, :] = dens.astype(BF16).astype(F32)
    row = lax.broadcasted_iota(jnp.int32, (fibres, 1), 0)
    owner = jnp.zeros((fibres, 1), jnp.int32)
    for f in range(fibres):
        owner = jnp.where(row == f, owner_ref[f], owner)
    points = points_ref[...]
    corner = [owner % 2, owner // 2 % 2, owner // 4]
    place = [
        points[:, c * nodes : (c + 1) * nodes] + (corner[c].astype(F32) - 1.0) for c in range(3)
    ]
    for f in range(fibres):
        lanes = slice(f * nodes, (f + 1) * nodes)
        for c in range(3):
            record_ref[0, c : c + 1, lanes] = place[c][f : f + 1, :]
    quad_weight = points[:, 3 * nodes :]
    rhs = rhs_ref[...]
    forces = jnp.zeros((fibres, quads), F32)
    for f in range(fibres):
        if f % part == 0:
            solves[f // part].wait()
        product = lax.dot_general(
            rhs, solve_ref[f], (((1,), (1,)), ((), ())), preferred_element_type=F32
        )
        forces = jnp.where(row == f, product, forces)
    pushes = forces * jnp.concatenate([quad_weight] * 4, axis=1)
    for f in range(fibres):
        lanes = slice(f * nodes, (f + 1) * nodes)
        for c in range(4):
            record_ref[1, c : c + 1, lanes] = pushes[f : f + 1, c * nodes : (c + 1) * nodes]
    lane = lax.broadcasted_iota(jnp.int32, (fibres, width), 1)
    sums = jnp.zeros((fibres, width), F32)
    for c in range(4):
        box_sum = jnp.sum(pushes[:, c * nodes : (c + 1) * nodes], axis=1, keepdims=True)
        sums = jnp.where(lane == owner + 8 * c, box_sum, sums)
    record_ref[0, 3:4, :] = jnp.sum(sums, axis=0, keepdims=True)


def prepare(fibre_solve, fibre_rhs, fibre_points, fibre_owner, density, shell_points):
    fibres, quads = fibre_points.shape
    width = fibres * quads // 4
    inputs = (
        fibre_solve,
        fibre_rhs,
        fibre_points,
        fibre_owner.reshape(fibres),
        density,
        shell_points,
    )
    return pl.pallas_call(
        prepare_kernel,
        out_shape=(
            jax.ShapeDtypeStruct((3, 4, width), F32),
            jax.ShapeDtypeStruct(shell_points.shape, F32),
        ),
        in_specs=[pl.BlockSpec(memory_space=pltpu.HBM)] * 6,
        out_specs=(VMEM, VMEM),
        scratch_shapes=[
            pltpu.VMEM(fibre_solve.shape, BF16),
            pltpu.VMEM(fibre_rhs.shape, BF16),
            pltpu.VMEM(fibre_points.shape, F32),
            pltpu.VMEM(density.shape, F32),
            pltpu.VMEM(shell_points.shape, F32),
            pltpu.SMEM((fibres,), jnp.int32),
            pltpu.SemaphoreType.DMA((fibres,)),
            pltpu.SemaphoreType.DMA((5,)),
        ],
        compiler_params=PARAMS,
        name="prepare",
    )(*[pltpu.with_memory_space_constraint(value, pltpu.HBM) for value in inputs])


def target_rows(place):
    sq = jnp.sum(place * place, axis=0, keepdims=True)
    high, middle, low = split3(place)
    one = jnp.ones_like(sq)
    zero = jnp.zeros_like(sq)
    sq_parts = split3(sq)
    return jnp.concatenate(
        [-2.0 * high, one] * 3
        + [-2.0 * middle, zero] * 2
        + [-2.0 * low, zero]
        + list(sq_parts)
        + [zero] * 5,
        axis=0,
    ).astype(BF16)


def source_rows(place):
    sq = jnp.sum(place * place, axis=0, keepdims=True) + smooth_sq
    high, middle, low = split3(jnp.concatenate([place, sq], axis=0))
    one = jnp.ones((3, place.shape[1]), F32)
    zero = jnp.zeros((5, place.shape[1]), F32)
    return jnp.concatenate([high, middle, low, high, middle, high, one, zero], axis=0).astype(BF16)


def source_terms(place, push, source):
    sq = jnp.sum(place * place, axis=0, keepdims=True) + 2.0 * smooth_sq
    rest = source - jnp.sum(place * push, axis=0, keepdims=True)
    terms = jnp.concatenate(
        [push, rest, sq * push - rest * place] + [place[a : a + 1] * push for a in range(3)], axis=0
    )
    return jnp.concatenate(split3(terms), axis=0).astype(BF16)


def add_sources(target_ref, groups, total_ref, block):
    targets = target_ref.shape[1]
    lead = total_ref.shape[0] // 3
    totals = {}
    for rows, terms in groups:
        width = rows.shape[1]
        step = min(block, width)
        for t in range(0, targets, block):
            for s in range(0, width, step):
                d = lax.dot_general(
                    rows[:, s : s + step],
                    target_ref[:, t : t + block],
                    (((0,), (0,)), ((), ())),
                    preferred_element_type=F32,
                )
                inverse = lax.rsqrt(d)
                cube = inverse * inverse * inverse
                high = cube.astype(BF16)
                low = (cube - high.astype(F32)).astype(BF16)
                term = terms[:, s : s + step]
                part = jnp.dot(term, high, preferred_element_type=F32)
                rest = jnp.dot(term[:lead], low, preferred_element_type=F32)
                part = jnp.concatenate([part[:lead] + rest, part[lead:]], axis=0)
                totals[t] = totals[t] + part if t in totals else part
    for t, value in totals.items():
        total_ref[:, t : t + block] += value


def point_columns(points):
    count = points.shape[1]
    eye = lax.broadcasted_iota(jnp.int32, (count, count), 0) == lax.broadcasted_iota(
        jnp.int32, (count, count), 1
    )
    return [
        2.0 * jnp.sum(jnp.where(eye, points[c : c + 1], 0.0), axis=1, keepdims=True) - 1.0
        for c in range(3)
    ]


def direct(columns, place, push, source):
    offset = [columns[c] - place[c : c + 1] for c in range(3)]
    sq = offset[0] * offset[0] + offset[1] * offset[1] + offset[2] * offset[2]
    inverse = lax.rsqrt(sq + smooth_sq)
    cube = inverse * inverse * inverse
    along = source + (
        offset[0] * push[0:1] + offset[1] * push[1:2] + offset[2] * push[2:3]
    )
    spread = cube * (sq + 2.0 * smooth_sq)
    along = cube * along
    return [spread * push[c : c + 1] + along * offset[c] for c in range(3)]


def fold(value, lanes):
    total = value[:, :lanes]
    for at in range(lanes, value.shape[1], lanes):
        total = total + value[:, at : at + lanes]
    return total


def near_kernel(shift, leaves, first, *refs):
    if first:
        records_ref, own_ref, shell_ref, total_ref, shell_total_ref, target_ref, sum_ref = refs
    else:
        (records_ref, own_ref, shell_ref, total_in, shell_in) = refs[:5]
        total_ref, shell_total_ref, target_ref, sum_ref = refs[5:]
    target_ref[...] = target_rows(own_ref[0, 0:3, :])
    sum_ref[...] = jnp.zeros_like(sum_ref)
    if first:
        shell_total_ref[...] = jnp.zeros_like(shell_total_ref)
    else:
        shell_total_ref[...] = shell_in[...]
    columns = point_columns(shell_ref[...])
    if shift is not None:
        moved = (2 * shift(lax.axis_index("leaf"))).astype(F32)
    count = records_ref.shape[0]
    unroll = max(u for u in range(1, 5) if count % u == 0)

    def body(at, carry):
        groups = []
        for j in range(unroll):
            record = records_ref.at[at * unroll + j]
            place = record[0, 0:3, :]
            if shift is not None:
                axis = lax.broadcasted_iota(jnp.int32, place.shape, 0)
                place = place + jnp.where(axis == 0, moved, 0.0)
            push, source = record[1, 0:3, :], record[1, 3:4, :]
            groups.append((source_rows(place), source_terms(place, push, source)))
            for c, value in enumerate(direct(columns, place, push, source)):
                shell_total_ref[c] += fold(value, 128)
        add_sources(target_ref, groups, sum_ref, 256)
        return carry

    if shift is not None:
        there = lax.axis_index("leaf") + shift(lax.axis_index("leaf"))
        steps = jnp.where((there >= 0) & (there < leaves), count // unroll, 0)
        lax.fori_loop(0, steps, body, 0)
    elif count == unroll:
        body(0, 0)
    else:
        lax.fori_loop(0, count // unroll, body, 0)
    terms = sum_ref.shape[0] // 3
    total = sum_ref[0:terms] + sum_ref[terms : 2 * terms] + sum_ref[2 * terms :]
    total_ref[...] = total if first else total + total_in[...]


def near(records, own, shell_points, shift, totals):
    targets = own.shape[2]
    count = shell_points.shape[1]
    out = (
        jax.ShapeDtypeStruct((16, targets), F32),
        jax.ShapeDtypeStruct((3, count, 128), F32),
    )
    pairs = records.shape[0] * targets * targets
    return pl.pallas_call(
        functools.partial(near_kernel, shift, lax.axis_size("leaf"), totals is None),
        out_shape=out,
        in_specs=[VMEM] * (3 if totals is None else 5),
        out_specs=(VMEM, VMEM),
        scratch_shapes=[pltpu.VMEM((32, targets), BF16), pltpu.VMEM((48, targets), F32)],
        compiler_params=PARAMS,
        cost_estimate=pl.CostEstimate(
            flops=500 * pairs, bytes_accessed=records.size * 4, transcendentals=pairs
        ),
        name="near",
    )(records, own, shell_points, *(totals or ()))


def finish_kernel(
    order,
    leaves,
    own_ref,
    shell_ref,
    held_ref,
    block_ref,
    total_in,
    shell_in,
    flow_ref,
    shell_flow_ref,
    target_ref,
    sum_ref,
):
    leaf, octant = lax.axis_index("leaf"), lax.axis_index("oct")
    octants = len(order)
    turned = (leaf + 1) // 2 % 2
    boxes = -(-leaves * octants // 128) * 128
    moments = []
    for c in range(4):
        parts = []
        for j in range(leaves):
            split = held_ref[j // 2, 2 * octants].astype(F32)
            at = ((j % 2) * 4 + c) * octants
            parts.append(jnp.sum(split[0:3, at : at + octants], axis=0, keepdims=True))
        if boxes > leaves * octants:
            parts.append(jnp.zeros((1, boxes - leaves * octants), F32))
        moments.append(jnp.concatenate(parts, axis=1))
    box = lax.broadcasted_iota(jnp.int32, (1, boxes), 1)
    other = box // 8
    other = jnp.bitwise_xor(other, turned * (other // 2 % 2))
    away = jnp.bitwise_xor(other, leaf) - leaf
    far = (jnp.abs(away) >= 2) & (box < leaves * octants)
    away = jnp.where(far, away, 0)
    child = box % 8
    place = jnp.concatenate(
        [
            (2 * away + child % 2).astype(F32) - 0.5,
            (child // 2 % 2).astype(F32) - 0.5,
            (child // 4).astype(F32) - 0.5,
        ],
        axis=0,
    )
    push = jnp.where(far, jnp.concatenate(moments[0:3], axis=0), 0.0)
    source = jnp.where(far, moments[3], 0.0)
    x = own_ref[0, 0:3, :]
    target_ref[...] = target_rows(x)
    sum_ref[...] = jnp.zeros_like(sum_ref)
    groups = [(source_rows(place), source_terms(place, push, source))]
    add_sources(target_ref, groups, sum_ref, 256)
    terms = sum_ref.shape[0] // 3
    total = total_in[...] + (
        sum_ref[0:terms] + sum_ref[terms : 2 * terms] + sum_ref[2 * terms :]
    )
    push_sum, rest_sum, constant = total[0:3], total[3:4], total[4:7]
    cross = [total[7 + 3 * a : 10 + 3 * a] for a in range(3)]
    flow = (
        jnp.sum(x * x, axis=0, keepdims=True) * push_sum
        + constant
        + x * (jnp.sum(x * push_sum, axis=0, keepdims=True) + rest_sum)
    )
    for a in range(3):
        flow = flow - 2.0 * x[a : a + 1] * cross[a]
    across = [
        jnp.sum(x * cross[c], axis=0, keepdims=True) for c in range(3)
    ]
    flow_ref[...] = stokes_scale * (flow - jnp.concatenate(across, axis=0))
    columns = point_columns(shell_ref[...])
    shell = [
        jnp.sum(shell_in[c] + fold(value, 128), axis=1, keepdims=True)
        for c, value in enumerate(direct(columns, place, push, source))
    ]
    width = held_ref.shape[3]
    rows = block_ref.shape[2] // (leaves * octants * width)
    count = block_ref.shape[1]

    def body(at, sums):
        other = jnp.bitwise_xor(at, turned * (at // 2 % 2))
        for j in range(octants):
            dens = held_ref[at // 2, (at % 2) * octants + j].astype(F32)
            owner = jnp.bitwise_xor(other, leaf) * octants + jnp.bitwise_xor(octant, order[j])
            for r in range(rows):
                start = pl.multiple_of((owner * rows + r) * width, 128)
                sums = tuple(
                    sums[c] + block_ref[c, :, pl.ds(start, width)].astype(F32) * dens[r : r + 1]
                    for c in range(3)
                )
        return sums

    zero = jnp.zeros((count, width), F32)
    sums = lax.fori_loop(0, leaves, body, (zero, zero, zero))
    product = [jnp.sum(sums[c], axis=1, keepdims=True) for c in range(3)]
    eye = lax.broadcasted_iota(jnp.int32, (count, count), 0) == lax.broadcasted_iota(
        jnp.int32, (count, count), 1
    )
    for c in range(3):
        column = product[c] + stokes_scale * shell[c]
        shell_flow_ref[c : c + 1, :] = jnp.sum(jnp.where(eye, column, 0.0), axis=0, keepdims=True)


def finish(order, leaves, own, shell_points, held, shell_block, totals):
    targets = own.shape[2]
    return pl.pallas_call(
        functools.partial(finish_kernel, order, leaves),
        out_shape=(
            jax.ShapeDtypeStruct((3, targets), F32),
            jax.ShapeDtypeStruct(shell_points.shape, F32),
        ),
        in_specs=[VMEM] * 6,
        out_specs=(VMEM, VMEM),
        scratch_shapes=[pltpu.VMEM((32, targets), BF16), pltpu.VMEM((48, targets), F32)],
        compiler_params=PARAMS,
        name="finish",
    )(own, shell_points, held, shell_block, *totals)


def exchange(value, axis, bit):
    count = lax.axis_size(axis)
    return lax.ppermute(value, axis, [(i, i ^ bit) for i in range(count)])


def together(*values):
    return lax.optimization_barrier(values)


def shards(fibre_solve, fibre_rhs, fibre_points, fibre_owner, shell_points, shell_block, density):
    octants = lax.axis_size("oct")
    leaves = lax.axis_size("leaf")
    record, shell = prepare(
        fibre_solve, fibre_rhs, fibre_points, fibre_owner, density, shell_points
    )
    count, width = record.shape[1:]

    def inner_shift(leaf):
        return 1 - 2 * (leaf % 2)

    def outer_shift(leaf):
        return 2 * (leaf % 2) - 1

    records, order = record[None], [0]
    fresh, totals = records, None
    for bit in [1 << b for b in range(1, octants.bit_length() - 1)]:
        arrived = exchange(records, "oct", bit)
        order = order + [j ^ bit for j in order]
        totals = near(fresh, record, shell, None, totals)
        arrived, totals = together(arrived, totals)
        records, fresh = jnp.concatenate([records, arrived], axis=0), arrived
    inner = exchange(records, "leaf", 1)
    totals = near(fresh, record, shell, None, totals)
    inner, totals = together(inner, totals)
    half = records.shape[0]
    order = order + [j ^ 1 for j in order]
    arrived = exchange(jnp.concatenate([records, inner], axis=0), "oct", 1)
    totals = near(inner, record, shell, inner_shift, totals)
    arrived, totals = together(arrived, totals)
    late, late_inner = arrived[:half], arrived[half:]
    records = jnp.concatenate([records, late], axis=0)
    inner = jnp.concatenate([inner, late_inner], axis=0)
    dens = jnp.concatenate([records[:, 2], inner[:, 2]], axis=0).astype(BF16)
    moments = jnp.concatenate(
        [jnp.sum(part[:, 0, 3, : 4 * octants], axis=0)[None] for part in (records, inner)], axis=1
    )
    high = lax.reduce_precision(moments, 8, 7)
    middle = lax.reduce_precision(moments - high, 8, 7)
    low = lax.reduce_precision(moments - high - middle, 8, 7)
    parts = jnp.concatenate([high, middle, low], axis=0).astype(BF16)
    parts = jnp.pad(parts, ((0, count - 3), (0, width - parts.shape[1])))
    held = jnp.concatenate([dens, parts[None]], axis=0)[None]
    swaps = []
    for leaf in range(leaves):
        other = leaf + outer_shift(leaf)
        for o in range(octants):
            there = other * octants + o if 0 <= other < leaves else leaf * octants + (o ^ 1)
            swaps.append((leaf * octants + o, there))
    outer = lax.ppermute(records[:, :2], ("leaf", "oct"), swaps)
    across = lax.ppermute(held, ("leaf", "oct"), swaps)
    totals = near(late, record, shell, None, totals)
    totals = near(late_inner, record, shell, inner_shift, totals)
    across, outer, totals = together(across, outer, totals)
    relayed = exchange(across, "leaf", 1)
    totals = near(outer, record, shell, outer_shift, totals)
    direct_pair = (lax.axis_index("leaf") + 1) // 2 % 2 == 1
    held = jnp.concatenate([held, jnp.where(direct_pair, across, relayed)], axis=0)
    for bit in [1 << b for b in range(2, leaves.bit_length() - 1)]:
        held = jnp.concatenate([held, exchange(held, "leaf", bit)], axis=0)
    return finish(tuple(order), leaves, record, shell, held, shell_block, totals)


def solution(mesh):
    placed = (
        P(("leaf", "oct"), None, None),
        P(("leaf", "oct"), None),
        P(("leaf", "oct"), None),
        P(("leaf", "oct"), None),
        P(None, ("leaf", "oct")),
        P(None, ("leaf", "oct"), None),
        P(("leaf", "oct")),
    )
    return jax.shard_map(
        shards,
        mesh=mesh,
        in_specs=placed,
        out_specs=(P(None, ("leaf", "oct")), P(None, ("leaf", "oct"))),
        check_vma=False,
    )
```

```python
import functools
import math

import jax
import jax.numpy as jnp
from jax import lax
from jax.experimental import pallas as pl
from jax.experimental.pallas import tpu as pltpu
from jax.sharding import PartitionSpec as P

smooth_sq = 0.01
stokes_scale = 1.0 / (8.0 * math.pi)
F32 = jnp.float32
BF16 = jnp.bfloat16
VMEM = pl.BlockSpec(memory_space=pltpu.VMEM)
PARAMS = pltpu.CompilerParams(vmem_limit_bytes=40 * 2**20)


def split3(value):
    high = value.astype(BF16).astype(F32)
    rest = value - high
    middle = rest.astype(BF16).astype(F32)
    return high, middle, (rest - middle).astype(BF16).astype(F32)


def prepare_kernel(*refs):
    solve_hbm, rhs_hbm, points_hbm, owner_hbm, density_hbm, shell_hbm = refs[:6]
    record_ref, target_ref, column_ref = refs[6:9]
    solve_ref, rhs_ref, points_ref, density_ref, shell_ref, owner_ref, solve_sem, sem = refs[9:]
    fibres, quads = rhs_ref.shape
    nodes = quads // 4
    width = record_ref.shape[2]
    part = math.gcd(fibres, 4)
    copies = [
        pltpu.make_async_copy(owner_hbm, owner_ref, sem.at[0]),
        pltpu.make_async_copy(points_hbm, points_ref, sem.at[1]),
        pltpu.make_async_copy(rhs_hbm, rhs_ref, sem.at[2]),
        pltpu.make_async_copy(density_hbm, density_ref, sem.at[3]),
        pltpu.make_async_copy(shell_hbm, shell_ref, sem.at[4]),
    ]
    solves = [
        pltpu.make_async_copy(
            solve_hbm.at[pl.ds(f, part)], solve_ref.at[pl.ds(f, part)], solve_sem.at[f // part]
        )
        for f in range(0, fibres, part)
    ]
    for copy in copies + solves:
        copy.start()
    for copy in copies:
        copy.wait()
    record_ref[2] = jnp.zeros(record_ref.shape[1:], F32)
    for r in range(density_ref.shape[0] // width):
        dens = density_ref[r * width : (r + 1) * width].reshape(1, width)
        record_ref[2, r : r + 1, :] = dens.astype(BF16).astype(F32)
    row = lax.broadcasted_iota(jnp.int32, (fibres, 1), 0)
    owner = jnp.zeros((fibres, 1), jnp.int32)
    for f in range(fibres):
        owner = jnp.where(row == f, owner_ref[f], owner)
    points = points_ref[...]
    corner = [owner % 2, owner // 2 % 2, owner // 4]
    place = [
        points[:, c * nodes : (c + 1) * nodes] + (corner[c].astype(F32) - 1.0) for c in range(3)
    ]
    for f in range(fibres):
        lanes = slice(f * nodes, (f + 1) * nodes)
        for c in range(3):
            record_ref[0, c : c + 1, lanes] = place[c][f : f + 1, :]
    quad_weight = points[:, 3 * nodes :]
    rhs = rhs_ref[...]
    forces = jnp.zeros((fibres, quads), F32)
    for f in range(fibres):
        if f % part == 0:
            solves[f // part].wait()
        product = lax.dot_general(
            rhs, solve_ref[f], (((1,), (1,)), ((), ())), preferred_element_type=F32
        )
        forces = jnp.where(row == f, product, forces)
    pushes = forces * jnp.concatenate([quad_weight] * 4, axis=1)
    for f in range(fibres):
        lanes = slice(f * nodes, (f + 1) * nodes)
        for c in range(4):
            record_ref[1, c : c + 1, lanes] = pushes[f : f + 1, c * nodes : (c + 1) * nodes]
    lane = lax.broadcasted_iota(jnp.int32, (fibres, width), 1)
    sums = jnp.zeros((fibres, width), F32)
    for c in range(4):
        box_sum = jnp.sum(pushes[:, c * nodes : (c + 1) * nodes], axis=1, keepdims=True)
        sums = jnp.where(lane == owner + 8 * c, box_sum, sums)
    record_ref[0, 3:4, :] = jnp.sum(sums, axis=0, keepdims=True)
    target_ref[...] = target_rows(record_ref[0, 0:3, :])
    for c, column in enumerate(point_columns(shell_ref[...])):
        column_ref[c] = jnp.broadcast_to(column, column_ref.shape[1:])


def prepare(fibre_solve, fibre_rhs, fibre_points, fibre_owner, density, shell_points):
    fibres, quads = fibre_points.shape
    width = fibres * quads // 4
    inputs = (
        fibre_solve,
        fibre_rhs,
        fibre_points,
        fibre_owner.reshape(fibres),
        density,
        shell_points,
    )
    return pl.pallas_call(
        prepare_kernel,
        out_shape=(
            jax.ShapeDtypeStruct((3, 4, width), F32),
            jax.ShapeDtypeStruct((32, width), BF16),
            jax.ShapeDtypeStruct((3, shell_points.shape[1], 128), F32),
        ),
        in_specs=[pl.BlockSpec(memory_space=pltpu.HBM)] * 6,
        out_specs=(VMEM, VMEM, VMEM),
        scratch_shapes=[
            pltpu.VMEM(fibre_solve.shape, BF16),
            pltpu.VMEM(fibre_rhs.shape, BF16),
            pltpu.VMEM(fibre_points.shape, F32),
            pltpu.VMEM(density.shape, F32),
            pltpu.VMEM(shell_points.shape, F32),
            pltpu.SMEM((fibres,), jnp.int32),
            pltpu.SemaphoreType.DMA((fibres,)),
            pltpu.SemaphoreType.DMA((5,)),
        ],
        compiler_params=PARAMS,
        name="prepare",
    )(*[pltpu.with_memory_space_constraint(value, pltpu.HBM) for value in inputs])


def target_rows(place):
    sq = jnp.sum(place * place, axis=0, keepdims=True)
    high, middle, low = split3(place)
    one = jnp.ones_like(sq)
    zero = jnp.zeros_like(sq)
    sq_parts = split3(sq)
    return jnp.concatenate(
        [-2.0 * high, one] * 3
        + [-2.0 * middle, zero] * 2
        + [-2.0 * low, zero]
        + list(sq_parts)
        + [zero] * 5,
        axis=0,
    ).astype(BF16)


def source_rows(place):
    sq = jnp.sum(place * place, axis=0, keepdims=True) + smooth_sq
    high, middle, low = split3(jnp.concatenate([place, sq], axis=0))
    one = jnp.ones((3, place.shape[1]), F32)
    zero = jnp.zeros((5, place.shape[1]), F32)
    return jnp.concatenate([high, middle, low, high, middle, high, one, zero], axis=0).astype(BF16)


def source_terms(place, push, source):
    sq = jnp.sum(place * place, axis=0, keepdims=True) + 2.0 * smooth_sq
    rest = source - jnp.sum(place * push, axis=0, keepdims=True)
    terms = jnp.concatenate(
        [push, rest, sq * push - rest * place] + [place[a : a + 1] * push for a in range(3)], axis=0
    )
    return jnp.concatenate(split3(terms), axis=0).astype(BF16)


def sum_sources(target_ref, groups, block):
    totals = []
    for t in range(0, target_ref.shape[1], block):
        total = None
        for rows, terms in groups:
            width = rows.shape[1]
            lead = terms.shape[0] // 3
            step = min(block, width)
            for s in range(0, width, step):
                d = lax.dot_general(
                    rows[:, s : s + step],
                    target_ref[:, t : t + block],
                    (((0,), (0,)), ((), ())),
                    preferred_element_type=F32,
                )
                inverse = lax.rsqrt(d)
                cube = inverse * inverse * inverse
                high = cube.astype(BF16)
                low = (cube - high.astype(F32)).astype(BF16)
                term = terms[:, s : s + step]
                part = jnp.dot(term, high, preferred_element_type=F32)
                rest = jnp.dot(term[:lead], low, preferred_element_type=F32)
                part = jnp.concatenate([part[:lead] + rest, part[lead:]], axis=0)
                total = part if total is None else total + part
        totals.append(total[:lead] + total[lead : 2 * lead] + total[2 * lead :])
    return totals


def point_columns(points):
    count = points.shape[1]
    eye = lax.broadcasted_iota(jnp.int32, (count, count), 0) == lax.broadcasted_iota(
        jnp.int32, (count, count), 1
    )
    return [
        2.0 * jnp.sum(jnp.where(eye, points[c : c + 1], 0.0), axis=1, keepdims=True) - 1.0
        for c in range(3)
    ]


def direct(columns, place, push, source):
    offset = [columns[c] - place[c : c + 1] for c in range(3)]
    sq = offset[0] * offset[0] + offset[1] * offset[1] + offset[2] * offset[2]
    inverse = lax.rsqrt(sq + smooth_sq)
    cube = inverse * inverse * inverse
    along = source + (
        offset[0] * push[0:1] + offset[1] * push[1:2] + offset[2] * push[2:3]
    )
    spread = cube * (sq + 2.0 * smooth_sq)
    along = cube * along
    return [spread * push[c : c + 1] + along * offset[c] for c in range(3)]


def fold(value, lanes):
    total = value[:, :lanes]
    for at in range(lanes, value.shape[1], lanes):
        total = total + value[:, at : at + lanes]
    return total


def near_kernel(shift, leaves, first, *refs):
    records_ref, target_ref, column_ref = refs[:3]
    total_in, shell_in = (None, None) if first else refs[3:5]
    total_ref, shell_total_ref = refs[-2:]
    columns = [column_ref[c][:, 0:1] for c in range(3)]
    if shift is not None:
        leaf = lax.axis_index("leaf")
        moved = (2 * shift(leaf)).astype(F32)
    targets = target_ref.shape[1]
    block = min(256, targets)

    def run():
        groups = []
        shell = [None if first else shell_in[c] for c in range(3)]
        for j in range(records_ref.shape[0]):
            record = records_ref.at[j]
            place = record[0, 0:3, :]
            if shift is not None:
                axis = lax.broadcasted_iota(jnp.int32, place.shape, 0)
                place = place + jnp.where(axis == 0, moved, 0.0)
            push, source = record[1, 0:3, :], record[1, 3:4, :]
            groups.append((source_rows(place), source_terms(place, push, source)))
            for c, value in enumerate(direct(columns, place, push, source)):
                value = fold(value, 128)
                shell[c] = value if shell[c] is None else shell[c] + value
        for at, value in enumerate(sum_sources(target_ref, groups, block)):
            lanes = slice(at * block, (at + 1) * block)
            total_ref[:, lanes] = value if first else value + total_in[:, lanes]
        for c in range(3):
            shell_total_ref[c] = shell[c]

    if shift is None:
        run()
        return
    there = leaf + shift(leaf)
    inside = (there >= 0) & (there < leaves)
    pl.when(inside)(run)

    @pl.when(jnp.logical_not(inside))
    def _():
        total_ref[...] = total_in[...]
        shell_total_ref[...] = shell_in[...]


def near(records, own, shift, totals):
    target_rows, columns = own
    targets = target_rows.shape[1]
    out = (jax.ShapeDtypeStruct((16, targets), F32), jax.ShapeDtypeStruct(columns.shape, F32))
    pairs = records.shape[0] * records.shape[3] * targets
    return pl.pallas_call(
        functools.partial(near_kernel, shift, lax.axis_size("leaf"), totals is None),
        out_shape=out,
        in_specs=[VMEM] * (3 if totals is None else 5),
        out_specs=(VMEM, VMEM),
        compiler_params=PARAMS,
        cost_estimate=pl.CostEstimate(
            flops=500 * pairs, bytes_accessed=records.size * 4, transcendentals=pairs
        ),
        name="near",
    )(records, target_rows, columns, *(totals or ()))


def super_box(position, leaf):
    turned = (leaf + 1) // 2 % 2
    return jnp.bitwise_xor(jnp.bitwise_xor(position, turned * (position // 2 % 2)), leaf)


def block_product(order, leaves, first, held_ref, block_ref):
    leaf, octant = lax.axis_index("leaf"), lax.axis_index("oct")
    octants = len(order)
    width = held_ref.shape[3]
    rows = block_ref.shape[2] // (leaves * octants * width)
    count = block_ref.shape[1]

    def body(at, sums):
        position = at + first
        seat = jnp.bitwise_xor(octant, position // 2 % 2)
        box = super_box(position, leaf)
        for j in range(octants):
            dens = held_ref[at // 2, (at % 2) * octants + j].astype(F32)
            owner = box * octants + jnp.bitwise_xor(seat, order[j])
            for r in range(rows):
                start = pl.multiple_of((owner * rows + r) * width, 128)
                sums = tuple(
                    sums[c] + block_ref[c, :, pl.ds(start, width)].astype(F32) * dens[r : r + 1]
                    for c in range(3)
                )
        return sums

    zero = jnp.zeros((count, width), F32)
    steps = 2 * held_ref.shape[0]
    return lax.fori_loop(0, steps, body, (zero, zero, zero), unroll=steps <= 4)


def shell_rows_kernel(order, leaves, held_ref, block_ref, product_ref):
    for c, value in enumerate(block_product(order, leaves, 0, held_ref, block_ref)):
        product_ref[c] = fold(value, 128)


def shell_rows(order, leaves, held, shell_block):
    return pl.pallas_call(
        functools.partial(shell_rows_kernel, order, leaves),
        out_shape=jax.ShapeDtypeStruct((3, shell_block.shape[1], 128), F32),
        in_specs=[VMEM] * 2,
        out_specs=VMEM,
        compiler_params=PARAMS,
        name="shell_rows",
    )(held, shell_block)


def finish_kernel(
    order,
    leaves,
    own_ref,
    target_ref,
    column_ref,
    held_ref,
    block_ref,
    product_in,
    total_in,
    shell_in,
    flow_ref,
    shell_flow_ref,
):
    leaf = lax.axis_index("leaf")
    octants = len(order)
    used = 2 * held_ref.shape[0] * octants
    boxes = -(-used // 128) * 128
    moments = []
    for c in range(4):
        parts = []
        for j in range(2 * held_ref.shape[0]):
            split = held_ref[j // 2, 2 * octants].astype(F32)
            at = ((j % 2) * 4 + c) * octants
            parts.append(jnp.sum(split[0:3, at : at + octants], axis=0, keepdims=True))
        if boxes > used:
            parts.append(jnp.zeros((1, boxes - used), F32))
        moments.append(jnp.concatenate(parts, axis=1))
    box = lax.broadcasted_iota(jnp.int32, (1, boxes), 1)
    away = super_box(box // 8 + 2, leaf) - leaf
    far = (jnp.abs(away) >= 2) & (box < used)
    away = jnp.where(far, away, 0)
    child = box % 8
    place = jnp.concatenate(
        [
            (2 * away + child % 2).astype(F32) - 0.5,
            (child // 2 % 2).astype(F32) - 0.5,
            (child // 4).astype(F32) - 0.5,
        ],
        axis=0,
    )
    push = jnp.where(far, jnp.concatenate(moments[0:3], axis=0), 0.0)
    source = jnp.where(far, moments[3], 0.0)
    x = own_ref[0, 0:3, :]
    groups = [(source_rows(place), source_terms(place, push, source))]
    far_sums = sum_sources(target_ref, groups, min(256, x.shape[1]))
    total = total_in[...] + jnp.concatenate(far_sums, axis=1)
    push_sum, rest_sum, constant = total[0:3], total[3:4], total[4:7]
    cross = [total[7 + 3 * a : 10 + 3 * a] for a in range(3)]
    flow = (
        jnp.sum(x * x, axis=0, keepdims=True) * push_sum
        + constant
        + x * (jnp.sum(x * push_sum, axis=0, keepdims=True) + rest_sum)
    )
    for a in range(3):
        flow = flow - 2.0 * x[a : a + 1] * cross[a]
    across = [
        jnp.sum(x * cross[c], axis=0, keepdims=True) for c in range(3)
    ]
    flow_ref[...] = stokes_scale * (flow - jnp.concatenate(across, axis=0))
    columns = [column_ref[c][:, 0:1] for c in range(3)]
    shell = [
        jnp.sum(shell_in[c] + fold(value, 128), axis=1, keepdims=True)
        for c, value in enumerate(direct(columns, place, push, source))
    ]
    count = block_ref.shape[1]
    product = [
        jnp.sum(product_in[c] + fold(value, 128), axis=1, keepdims=True)
        for c, value in enumerate(block_product(order, leaves, 2, held_ref, block_ref))
    ]
    eye = lax.broadcasted_iota(jnp.int32, (count, count), 0) == lax.broadcasted_iota(
        jnp.int32, (count, count), 1
    )
    for c in range(3):
        column = product[c] + stokes_scale * shell[c]
        shell_flow_ref[c : c + 1, :] = jnp.sum(jnp.where(eye, column, 0.0), axis=0, keepdims=True)


def finish(order, leaves, record, own, held, shell_block, product, totals):
    targets, points = record.shape[2], shell_block.shape[1]
    return pl.pallas_call(
        functools.partial(finish_kernel, order, leaves),
        out_shape=(
            jax.ShapeDtypeStruct((3, targets), F32),
            jax.ShapeDtypeStruct((3, points), F32),
        ),
        in_specs=[VMEM] * 8,
        out_specs=(VMEM, VMEM),
        compiler_params=PARAMS,
        name="finish",
    )(record, *own, held, shell_block, product, *totals)


def exchange(value, bits):
    devices = lax.axis_size("leaf") * lax.axis_size("oct")
    return lax.ppermute(value, ("leaf", "oct"), [(i, i ^ bits) for i in range(devices)])


def together(*values):
    return lax.optimization_barrier(values)


def shards(fibre_solve, fibre_rhs, fibre_points, fibre_owner, shell_points, shell_block, density):
    octants = lax.axis_size("oct")
    leaves = lax.axis_size("leaf")
    record, *own = prepare(
        fibre_solve, fibre_rhs, fibre_points, fibre_owner, density, shell_points
    )
    count, width = record.shape[1:]

    def inner_shift(leaf):
        return 1 - 2 * (leaf % 2)

    def outer_shift(leaf):
        return 2 * (leaf % 2) - 1

    order = [0]
    for bit in [1 << b for b in range(1, octants.bit_length() - 1)]:
        order = order + [j ^ bit ^ 1 for j in order]
    arrived = [exchange(record, j) for j in order[1:]]
    totals = near(record[None], own, None, None)
    *arrived, totals = together(*arrived, totals)
    fresh = jnp.stack(arrived)
    records = jnp.stack([record] + arrived)
    swaps = []
    for leaf in range(leaves):
        there = leaf + outer_shift(leaf)
        there = there if 0 <= there < leaves else leaf
        swaps += [(leaf * octants + o, there * octants + (o ^ 1)) for o in range(octants)]
    order = order + [j ^ 1 for j in order]
    inner = exchange(records, octants + 1)
    late = exchange(records, 1)
    totals = near(fresh, own, None, totals)
    late, totals = together(late, totals)
    records = jnp.concatenate([records, late], axis=0)
    outer = lax.ppermute(records[:, :2], ("leaf", "oct"), swaps)
    totals = near(late, own, None, totals)
    inner, totals = together(inner, totals)
    late_inner = exchange(inner, 1)
    totals = near(inner, own, inner_shift, totals)
    late_inner, totals = together(late_inner, totals)
    inner = jnp.concatenate([late_inner, inner], axis=0)
    dens = jnp.concatenate([records[:, 2], inner[:, 2]], axis=0).astype(BF16)
    moments = jnp.concatenate(
        [jnp.sum(part[:, 0, 3, : 4 * octants], axis=0)[None] for part in (records, inner)], axis=1
    )
    high = lax.reduce_precision(moments, 8, 7)
    middle = lax.reduce_precision(moments - high, 8, 7)
    low = lax.reduce_precision(moments - high - middle, 8, 7)
    parts = jnp.concatenate([high, middle, low], axis=0).astype(BF16)
    parts = jnp.pad(parts, ((0, count - 3), (0, width - parts.shape[1])))
    held = jnp.concatenate([dens, parts[None]], axis=0)[None]
    across = lax.ppermute(held, ("leaf", "oct"), swaps)
    totals = near(late_inner, own, inner_shift, totals)
    held, totals = together(held, totals)
    product = shell_rows(tuple(order), leaves, held, shell_block)
    across, product, totals = together(across, product, totals)
    relayed = exchange(across, octants)
    totals = near(outer, own, outer_shift, totals)
    straight = (lax.axis_index("leaf") + 1) // 2 % 2 == 1
    rest = jnp.where(straight, across, relayed)
    for bit in [1 << b for b in range(2, leaves.bit_length() - 1)]:
        whole = jnp.concatenate([held, rest], axis=0)
        rest = jnp.concatenate([rest, exchange(whole, bit * octants)], axis=0)
    return finish(tuple(order), leaves, record, own, rest, shell_block, product, totals)


def solution(mesh):
    placed = (
        P(("leaf", "oct"), None, None),
        P(("leaf", "oct"), None),
        P(("leaf", "oct"), None),
        P(("leaf", "oct"), None),
        P(None, ("leaf", "oct")),
        P(None, ("leaf", "oct"), None),
        P(("leaf", "oct")),
    )
    return jax.shard_map(
        shards,
        mesh=mesh,
        in_specs=placed,
        out_specs=(P(None, ("leaf", "oct")), P(None, ("leaf", "oct"))),
        check_vma=False,
    )
```

```python
import functools
import math

import jax
import jax.numpy as jnp
from jax import lax
from jax.experimental import pallas as pl
from jax.experimental.pallas import tpu as pltpu
from jax.sharding import PartitionSpec as P

smooth_sq = 0.01
stokes_scale = 1.0 / (8.0 * math.pi)
F32 = jnp.float32
BF16 = jnp.bfloat16
VMEM = pl.BlockSpec(memory_space=pltpu.VMEM)
PARAMS = pltpu.CompilerParams(vmem_limit_bytes=40 * 2**20)


def split3(value):
    high = value.astype(BF16).astype(F32)
    rest = value - high
    middle = rest.astype(BF16).astype(F32)
    return high, middle, (rest - middle).astype(BF16).astype(F32)


def prepare_kernel(*refs):
    solve_hbm, rhs_hbm, points_hbm, owner_hbm, density_hbm, shell_hbm = refs[:6]
    record_ref, target_ref, column_ref = refs[6:9]
    solve_ref, rhs_ref, points_ref, density_ref, shell_ref, owner_ref, solve_sem, sem = refs[9:]
    fibres, quads = rhs_ref.shape
    nodes = quads // 4
    width = record_ref.shape[2]
    part = math.gcd(fibres, 4)
    copies = [
        pltpu.make_async_copy(owner_hbm, owner_ref, sem.at[0]),
        pltpu.make_async_copy(points_hbm, points_ref, sem.at[1]),
        pltpu.make_async_copy(rhs_hbm, rhs_ref, sem.at[2]),
        pltpu.make_async_copy(density_hbm, density_ref, sem.at[3]),
        pltpu.make_async_copy(shell_hbm, shell_ref, sem.at[4]),
    ]
    solves = [
        pltpu.make_async_copy(
            solve_hbm.at[pl.ds(f, part)], solve_ref.at[pl.ds(f, part)], solve_sem.at[f // part]
        )
        for f in range(0, fibres, part)
    ]
    for copy in copies + solves:
        copy.start()
    for copy in copies:
        copy.wait()
    record_ref[2] = jnp.zeros(record_ref.shape[1:], F32)
    for r in range(density_ref.shape[0] // width):
        dens = density_ref[r * width : (r + 1) * width].reshape(1, width)
        record_ref[2, r : r + 1, :] = dens.astype(BF16).astype(F32)
    row = lax.broadcasted_iota(jnp.int32, (fibres, 1), 0)
    owner = jnp.zeros((fibres, 1), jnp.int32)
    for f in range(fibres):
        owner = jnp.where(row == f, owner_ref[f], owner)
    points = points_ref[...]
    corner = [owner % 2, owner // 2 % 2, owner // 4]
    place = [
        points[:, c * nodes : (c + 1) * nodes] + (corner[c].astype(F32) - 1.0) for c in range(3)
    ]
    for f in range(fibres):
        lanes = slice(f * nodes, (f + 1) * nodes)
        for c in range(3):
            record_ref[0, c : c + 1, lanes] = place[c][f : f + 1, :]
    quad_weight = points[:, 3 * nodes :]
    rhs = rhs_ref[...]
    forces = jnp.zeros((fibres, quads), F32)
    for f in range(fibres):
        if f % part == 0:
            solves[f // part].wait()
        product = lax.dot_general(
            rhs, solve_ref[f], (((1,), (1,)), ((), ())), preferred_element_type=F32
        )
        forces = jnp.where(row == f, product, forces)
    pushes = forces * jnp.concatenate([quad_weight] * 4, axis=1)
    for f in range(fibres):
        lanes = slice(f * nodes, (f + 1) * nodes)
        for c in range(4):
            record_ref[1, c : c + 1, lanes] = pushes[f : f + 1, c * nodes : (c + 1) * nodes]
    lane = lax.broadcasted_iota(jnp.int32, (fibres, width), 1)
    sums = jnp.zeros((fibres, width), F32)
    for c in range(4):
        box_sum = jnp.sum(pushes[:, c * nodes : (c + 1) * nodes], axis=1, keepdims=True)
        sums = jnp.where(lane == owner + 8 * c, box_sum, sums)
    record_ref[0, 3:4, :] = jnp.sum(sums, axis=0, keepdims=True)
    target_ref[...] = target_rows(record_ref[0, 0:3, :])
    for c, column in enumerate(point_columns(shell_ref[...])):
        column_ref[c] = jnp.broadcast_to(column, column_ref.shape[1:])


def prepare(fibre_solve, fibre_rhs, fibre_points, fibre_owner, density, shell_points):
    fibres, quads = fibre_points.shape
    width = fibres * quads // 4
    inputs = (
        fibre_solve,
        fibre_rhs,
        fibre_points,
        fibre_owner.reshape(fibres),
        density,
        shell_points,
    )
    return pl.pallas_call(
        prepare_kernel,
        out_shape=(
            jax.ShapeDtypeStruct((3, 4, width), F32),
            jax.ShapeDtypeStruct((32, width), BF16),
            jax.ShapeDtypeStruct((3, shell_points.shape[1], 128), F32),
        ),
        in_specs=[pl.BlockSpec(memory_space=pltpu.HBM)] * 6,
        out_specs=(VMEM, VMEM, VMEM),
        scratch_shapes=[
            pltpu.VMEM(fibre_solve.shape, BF16),
            pltpu.VMEM(fibre_rhs.shape, BF16),
            pltpu.VMEM(fibre_points.shape, F32),
            pltpu.VMEM(density.shape, F32),
            pltpu.VMEM(shell_points.shape, F32),
            pltpu.SMEM((fibres,), jnp.int32),
            pltpu.SemaphoreType.DMA((fibres,)),
            pltpu.SemaphoreType.DMA((5,)),
        ],
        compiler_params=PARAMS,
        name="prepare",
    )(*[pltpu.with_memory_space_constraint(value, pltpu.HBM) for value in inputs])


def target_rows(place):
    sq = jnp.sum(place * place, axis=0, keepdims=True)
    high, middle, low = split3(place)
    one = jnp.ones_like(sq)
    zero = jnp.zeros_like(sq)
    sq_parts = split3(sq)
    return jnp.concatenate(
        [-2.0 * high, one] * 3
        + [-2.0 * middle, zero] * 2
        + [-2.0 * low, zero]
        + list(sq_parts)
        + [zero] * 5,
        axis=0,
    ).astype(BF16)


def source_rows(place):
    sq = jnp.sum(place * place, axis=0, keepdims=True) + smooth_sq
    high, middle, low = split3(jnp.concatenate([place, sq], axis=0))
    one = jnp.ones((3, place.shape[1]), F32)
    zero = jnp.zeros((5, place.shape[1]), F32)
    return jnp.concatenate([high, middle, low, high, middle, high, one, zero], axis=0).astype(BF16)


def source_terms(place, push, source):
    sq = jnp.sum(place * place, axis=0, keepdims=True) + 2.0 * smooth_sq
    rest = source - jnp.sum(place * push, axis=0, keepdims=True)
    terms = jnp.concatenate(
        [push, rest, sq * push - rest * place] + [place[a : a + 1] * push for a in range(3)], axis=0
    )
    return jnp.concatenate(split3(terms), axis=0).astype(BF16)


def sum_sources(target_ref, groups, block):
    totals = []
    for t in range(0, target_ref.shape[1], block):
        total = None
        for rows, terms in groups:
            width = rows.shape[1]
            lead = terms.shape[0] // 3
            step = min(block, width)
            for s in range(0, width, step):
                d = lax.dot_general(
                    rows[:, s : s + step],
                    target_ref[:, t : t + block],
                    (((0,), (0,)), ((), ())),
                    preferred_element_type=F32,
                )
                inverse = lax.rsqrt(d)
                cube = inverse * inverse * inverse
                high = cube.astype(BF16)
                low = (cube - high.astype(F32)).astype(BF16)
                term = terms[:, s : s + step]
                part = jnp.dot(term, high, preferred_element_type=F32)
                rest = jnp.dot(term[:lead], low, preferred_element_type=F32)
                part = jnp.concatenate([part[:lead] + rest, part[lead:]], axis=0)
                total = part if total is None else total + part
        totals.append(total[:lead] + total[lead : 2 * lead] + total[2 * lead :])
    return totals


def point_columns(points):
    count = points.shape[1]
    eye = lax.broadcasted_iota(jnp.int32, (count, count), 0) == lax.broadcasted_iota(
        jnp.int32, (count, count), 1
    )
    return [
        2.0 * jnp.sum(jnp.where(eye, points[c : c + 1], 0.0), axis=1, keepdims=True) - 1.0
        for c in range(3)
    ]


def direct(columns, place, push, source):
    offset = [columns[c] - place[c : c + 1] for c in range(3)]
    sq = offset[0] * offset[0] + offset[1] * offset[1] + offset[2] * offset[2]
    inverse = lax.rsqrt(sq + smooth_sq)
    cube = inverse * inverse * inverse
    along = source + (
        offset[0] * push[0:1] + offset[1] * push[1:2] + offset[2] * push[2:3]
    )
    spread = cube * (sq + 2.0 * smooth_sq)
    along = cube * along
    return [spread * push[c : c + 1] + along * offset[c] for c in range(3)]


def fold(value, lanes):
    total = value[:, :lanes]
    for at in range(lanes, value.shape[1], lanes):
        total = total + value[:, at : at + lanes]
    return total


def near_kernel(shift, leaves, first, *refs):
    records_ref, target_ref, column_ref = refs[:3]
    total_in, shell_in = (None, None) if first else refs[3:5]
    total_ref, shell_total_ref = refs[-2:]
    columns = [column_ref[c][:, 0:1] for c in range(3)]
    if shift is not None:
        leaf = lax.axis_index("leaf")
        moved = (2 * shift(leaf)).astype(F32)
    targets = target_ref.shape[1]
    block = min(256, targets)

    def run():
        groups = []
        shell = [None if first else shell_in[c] for c in range(3)]
        for j in range(records_ref.shape[0]):
            record = records_ref.at[j]
            place = record[0, 0:3, :]
            if shift is not None:
                axis = lax.broadcasted_iota(jnp.int32, place.shape, 0)
                place = place + jnp.where(axis == 0, moved, 0.0)
            push, source = record[1, 0:3, :], record[1, 3:4, :]
            groups.append((source_rows(place), source_terms(place, push, source)))
            for c, value in enumerate(direct(columns, place, push, source)):
                value = fold(value, 128)
                shell[c] = value if shell[c] is None else shell[c] + value
        for at, value in enumerate(sum_sources(target_ref, groups, block)):
            lanes = slice(at * block, (at + 1) * block)
            total_ref[:, lanes] = value if first else value + total_in[:, lanes]
        for c in range(3):
            shell_total_ref[c] = shell[c]

    if shift is None:
        run()
        return
    there = leaf + shift(leaf)
    inside = (there >= 0) & (there < leaves)
    pl.when(inside)(run)

    @pl.when(jnp.logical_not(inside))
    def _():
        total_ref[...] = total_in[...]
        shell_total_ref[...] = shell_in[...]


def near(records, own, shift, totals):
    target_rows, columns = own
    targets = target_rows.shape[1]
    out = (jax.ShapeDtypeStruct((16, targets), F32), jax.ShapeDtypeStruct(columns.shape, F32))
    pairs = records.shape[0] * records.shape[3] * targets
    return pl.pallas_call(
        functools.partial(near_kernel, shift, lax.axis_size("leaf"), totals is None),
        out_shape=out,
        in_specs=[VMEM] * (3 if totals is None else 5),
        out_specs=(VMEM, VMEM),
        compiler_params=PARAMS,
        cost_estimate=pl.CostEstimate(
            flops=500 * pairs, bytes_accessed=records.size * 4, transcendentals=pairs
        ),
        name="near",
    )(records, target_rows, columns, *(totals or ()))


def block_product(order, leaves, first, held_ref, block_ref):
    leaf, octant = lax.axis_index("leaf"), lax.axis_index("oct")
    octants = len(order)
    width = held_ref.shape[3]
    rows = block_ref.shape[2] // (leaves * octants * width)
    count = block_ref.shape[1]

    def body(at, sums):
        position = at + first
        seat = jnp.bitwise_xor(octant, position // 2 % 2)
        box = jnp.bitwise_xor(position, leaf)
        for j in range(octants):
            dens = held_ref[at // 2, (at % 2) * octants + j].astype(F32)
            owner = box * octants + jnp.bitwise_xor(seat, order[j])
            for r in range(rows):
                start = pl.multiple_of((owner * rows + r) * width, 128)
                sums = tuple(
                    sums[c] + block_ref[c, :, pl.ds(start, width)].astype(F32) * dens[r : r + 1]
                    for c in range(3)
                )
        return sums

    zero = jnp.zeros((count, width), F32)
    steps = 2 * held_ref.shape[0]
    return lax.fori_loop(0, steps, body, (zero, zero, zero), unroll=steps <= 4)


def shell_rows_kernel(order, leaves, held_ref, block_ref, product_ref):
    for c, value in enumerate(block_product(order, leaves, 0, held_ref, block_ref)):
        product_ref[c] = fold(value, 128)


def shell_rows(order, leaves, held, shell_block):
    return pl.pallas_call(
        functools.partial(shell_rows_kernel, order, leaves),
        out_shape=jax.ShapeDtypeStruct((3, shell_block.shape[1], 128), F32),
        in_specs=[VMEM] * 2,
        out_specs=VMEM,
        compiler_params=PARAMS,
        name="shell_rows",
    )(held, shell_block)


def finish_kernel(
    order,
    leaves,
    own_ref,
    target_ref,
    column_ref,
    held_ref,
    block_ref,
    product_in,
    total_in,
    shell_in,
    flow_ref,
    shell_flow_ref,
):
    leaf = lax.axis_index("leaf")
    octants = len(order)
    used = 2 * held_ref.shape[0] * octants
    boxes = -(-used // 128) * 128
    moments = []
    for c in range(4):
        parts = []
        for j in range(2 * held_ref.shape[0]):
            split = held_ref[j // 2, 2 * octants].astype(F32)
            at = ((j % 2) * 4 + c) * octants
            parts.append(jnp.sum(split[0:3, at : at + octants], axis=0, keepdims=True))
        if boxes > used:
            parts.append(jnp.zeros((1, boxes - used), F32))
        moments.append(jnp.concatenate(parts, axis=1))
    box = lax.broadcasted_iota(jnp.int32, (1, boxes), 1)
    away = jnp.bitwise_xor(box // 8 + 2, leaf) - leaf
    far = (jnp.abs(away) >= 2) & (box < used)
    away = jnp.where(far, away, 0)
    child = box % 8
    place = jnp.concatenate(
        [
            (2 * away + child % 2).astype(F32) - 0.5,
            (child // 2 % 2).astype(F32) - 0.5,
            (child // 4).astype(F32) - 0.5,
        ],
        axis=0,
    )
    push = jnp.where(far, jnp.concatenate(moments[0:3], axis=0), 0.0)
    source = jnp.where(far, moments[3], 0.0)
    x = own_ref[0, 0:3, :]
    groups = [(source_rows(place), source_terms(place, push, source))]
    far_sums = sum_sources(target_ref, groups, min(256, x.shape[1]))
    total = total_in[...] + jnp.concatenate(far_sums, axis=1)
    push_sum, rest_sum, constant = total[0:3], total[3:4], total[4:7]
    cross = [total[7 + 3 * a : 10 + 3 * a] for a in range(3)]
    flow = (
        jnp.sum(x * x, axis=0, keepdims=True) * push_sum
        + constant
        + x * (jnp.sum(x * push_sum, axis=0, keepdims=True) + rest_sum)
    )
    for a in range(3):
        flow = flow - 2.0 * x[a : a + 1] * cross[a]
    across = [
        jnp.sum(x * cross[c], axis=0, keepdims=True) for c in range(3)
    ]
    flow_ref[...] = stokes_scale * (flow - jnp.concatenate(across, axis=0))
    columns = [column_ref[c][:, 0:1] for c in range(3)]
    shell = [
        jnp.sum(shell_in[c] + fold(value, 128), axis=1, keepdims=True)
        for c, value in enumerate(direct(columns, place, push, source))
    ]
    count = block_ref.shape[1]
    product = [
        jnp.sum(product_in[c] + fold(value, 128), axis=1, keepdims=True)
        for c, value in enumerate(block_product(order, leaves, 2, held_ref, block_ref))
    ]
    eye = lax.broadcasted_iota(jnp.int32, (count, count), 0) == lax.broadcasted_iota(
        jnp.int32, (count, count), 1
    )
    for c in range(3):
        column = product[c] + stokes_scale * shell[c]
        shell_flow_ref[c : c + 1, :] = jnp.sum(jnp.where(eye, column, 0.0), axis=0, keepdims=True)


def finish(order, leaves, record, own, held, shell_block, product, totals):
    targets, points = record.shape[2], shell_block.shape[1]
    return pl.pallas_call(
        functools.partial(finish_kernel, order, leaves),
        out_shape=(
            jax.ShapeDtypeStruct((3, targets), F32),
            jax.ShapeDtypeStruct((3, points), F32),
        ),
        in_specs=[VMEM] * 8,
        out_specs=(VMEM, VMEM),
        compiler_params=PARAMS,
        name="finish",
    )(record, *own, held, shell_block, product, *totals)


def exchange(value, bits):
    devices = lax.axis_size("leaf") * lax.axis_size("oct")
    return lax.ppermute(value, ("leaf", "oct"), [(i, i ^ bits) for i in range(devices)])


def together(*values):
    return lax.optimization_barrier(values)


def shards(fibre_solve, fibre_rhs, fibre_points, fibre_owner, shell_points, shell_block, density):
    octants = lax.axis_size("oct")
    leaves = lax.axis_size("leaf")
    record, *own = prepare(
        fibre_solve, fibre_rhs, fibre_points, fibre_owner, density, shell_points
    )
    count, width = record.shape[1:]

    def inner_shift(leaf):
        return 1 - 2 * (leaf % 2)

    def outer_shift(leaf):
        return 2 * (leaf % 2) - 1

    order = [0]
    for bit in [1 << b for b in range(1, octants.bit_length() - 1)]:
        order = order + [j ^ bit ^ 1 for j in order]
    arrived = [exchange(record, j) for j in order[:0:-1]][::-1]
    totals = near(record[None], own, None, None)
    *arrived, totals = together(*arrived[::-1], totals)
    arrived = arrived[::-1]
    fresh = jnp.stack(arrived)
    records = jnp.stack([record] + arrived)
    swaps = []
    for leaf in range(leaves):
        there = leaf + outer_shift(leaf)
        there = there if 0 <= there < leaves else leaf
        swaps += [(leaf * octants + o, there * octants + (o ^ 1)) for o in range(octants)]
    order = order + [j ^ 1 for j in order]
    inner = exchange(records, octants + 1)
    outer = lax.ppermute(records[:, :2], ("leaf", "oct"), swaps)
    late = exchange(records, 1)
    totals = near(fresh, own, None, totals)
    late, totals = together(late, totals)
    records = jnp.concatenate([records, late], axis=0)
    totals = near(late, own, None, totals)
    outer, inner, totals = together(outer, inner, totals)
    late_inner, late_outer = exchange(inner, 1), exchange(outer, 1)
    totals = near(inner, own, inner_shift, totals)
    late_inner, late_outer, totals = together(late_inner, late_outer, totals)
    outer = jnp.concatenate([outer, late_outer], axis=0)
    inner = jnp.concatenate([late_inner, inner], axis=0)
    dens = jnp.concatenate([records[:, 2], inner[:, 2]], axis=0).astype(BF16)
    moments = jnp.concatenate(
        [jnp.sum(part[:, 0, 3, : 4 * octants], axis=0)[None] for part in (records, inner)], axis=1
    )
    high = lax.reduce_precision(moments, 8, 7)
    middle = lax.reduce_precision(moments - high, 8, 7)
    low = lax.reduce_precision(moments - high - middle, 8, 7)
    parts = jnp.concatenate([high, middle, low], axis=0).astype(BF16)
    parts = jnp.pad(parts, ((0, count - 3), (0, width - parts.shape[1])))
    held = jnp.concatenate([dens, parts[None]], axis=0)[None]
    bits = [(1 << b) * octants for b in range(1, leaves.bit_length() - 1)]
    rest = exchange(held, bits[0] + 1)
    totals = near(late_inner, own, inner_shift, totals)
    held, totals = together(held, totals)
    product = shell_rows(tuple(order), leaves, held, shell_block)
    product, totals = together(product, totals)
    totals = near(outer, own, outer_shift, totals)
    for bit in bits[1:]:
        whole = jnp.concatenate([held, rest], axis=0)
        rest = jnp.concatenate([rest, exchange(whole, bit)], axis=0)
    return finish(tuple(order), leaves, record, own, rest, shell_block, product, totals)


def solution(mesh):
    placed = (
        P(("leaf", "oct"), None, None),
        P(("leaf", "oct"), None),
        P(("leaf", "oct"), None),
        P(("leaf", "oct"), None),
        P(None, ("leaf", "oct")),
        P(None, ("leaf", "oct"), None),
        P(("leaf", "oct")),
    )
    return jax.shard_map(
        shards,
        mesh=mesh,
        in_specs=placed,
        out_specs=(P(None, ("leaf", "oct")), P(None, ("leaf", "oct"))),
        check_vma=False,
    )
```

```python
import functools
import math

import jax
import jax.numpy as jnp
from jax import lax
from jax.experimental import pallas as pl
from jax.experimental.pallas import tpu as pltpu
from jax.sharding import PartitionSpec as P

smooth_sq = 0.01
stokes_scale = 1.0 / (8.0 * math.pi)
F32 = jnp.float32
BF16 = jnp.bfloat16
VMEM = pl.BlockSpec(memory_space=pltpu.VMEM)
PARAMS = pltpu.CompilerParams(vmem_limit_bytes=40 * 2**20)


def split3(value):
    high = value.astype(BF16).astype(F32)
    rest = value - high
    middle = rest.astype(BF16).astype(F32)
    return high, middle, (rest - middle).astype(BF16).astype(F32)


def prepare_kernel(*refs):
    solve_hbm, rhs_hbm, points_hbm, owner_hbm, density_hbm, shell_hbm = refs[:6]
    record_ref, target_ref, column_ref = refs[6:9]
    solve_ref, rhs_ref, points_ref, density_ref, shell_ref, owner_ref, solve_sem, sem = refs[9:]
    fibres, quads = rhs_ref.shape
    nodes = quads // 4
    width = record_ref.shape[2]
    part = math.gcd(fibres, 4)
    copies = [
        pltpu.make_async_copy(owner_hbm, owner_ref, sem.at[0]),
        pltpu.make_async_copy(points_hbm, points_ref, sem.at[1]),
        pltpu.make_async_copy(rhs_hbm, rhs_ref, sem.at[2]),
        pltpu.make_async_copy(density_hbm, density_ref, sem.at[3]),
        pltpu.make_async_copy(shell_hbm, shell_ref, sem.at[4]),
    ]
    solves = [
        pltpu.make_async_copy(
            solve_hbm.at[pl.ds(f, part)], solve_ref.at[pl.ds(f, part)], solve_sem.at[f // part]
        )
        for f in range(0, fibres, part)
    ]
    for copy in copies + solves:
        copy.start()
    for copy in copies:
        copy.wait()
    record_ref[2] = jnp.zeros(record_ref.shape[1:], F32)
    for r in range(density_ref.shape[0] // width):
        dens = density_ref[r * width : (r + 1) * width].reshape(1, width)
        record_ref[2, r : r + 1, :] = dens.astype(BF16).astype(F32)
    row = lax.broadcasted_iota(jnp.int32, (fibres, 1), 0)
    owner = jnp.zeros((fibres, 1), jnp.int32)
    for f in range(fibres):
        owner = jnp.where(row == f, owner_ref[f], owner)
    points = points_ref[...]
    corner = [owner % 2, owner // 2 % 2, owner // 4]
    place = [
        points[:, c * nodes : (c + 1) * nodes] + (corner[c].astype(F32) - 1.0) for c in range(3)
    ]
    for f in range(fibres):
        lanes = slice(f * nodes, (f + 1) * nodes)
        for c in range(3):
            record_ref[0, c : c + 1, lanes] = place[c][f : f + 1, :]
    quad_weight = points[:, 3 * nodes :]
    rhs = rhs_ref[...]
    forces = jnp.zeros((fibres, quads), F32)
    for f in range(fibres):
        if f % part == 0:
            solves[f // part].wait()
        product = lax.dot_general(
            rhs, solve_ref[f], (((1,), (1,)), ((), ())), preferred_element_type=F32
        )
        forces = jnp.where(row == f, product, forces)
    pushes = forces * jnp.concatenate([quad_weight] * 4, axis=1)
    for f in range(fibres):
        lanes = slice(f * nodes, (f + 1) * nodes)
        for c in range(4):
            record_ref[1, c : c + 1, lanes] = pushes[f : f + 1, c * nodes : (c + 1) * nodes]
    lane = lax.broadcasted_iota(jnp.int32, (fibres, width), 1)
    sums = jnp.zeros((fibres, width), F32)
    for c in range(4):
        box_sum = jnp.sum(pushes[:, c * nodes : (c + 1) * nodes], axis=1, keepdims=True)
        sums = jnp.where(lane == owner + 8 * c, box_sum, sums)
    record_ref[0, 3:4, :] = jnp.sum(sums, axis=0, keepdims=True)
    target_ref[...] = target_rows(record_ref[0, 0:3, :])
    for c, column in enumerate(point_columns(shell_ref[...])):
        column_ref[c] = jnp.broadcast_to(column, column_ref.shape[1:])


def prepare(fibre_solve, fibre_rhs, fibre_points, fibre_owner, density, shell_points):
    fibres, quads = fibre_points.shape
    width = fibres * quads // 4
    inputs = (
        fibre_solve,
        fibre_rhs,
        fibre_points,
        fibre_owner.reshape(fibres),
        density,
        shell_points,
    )
    return pl.pallas_call(
        prepare_kernel,
        out_shape=(
            jax.ShapeDtypeStruct((3, 4, width), F32),
            jax.ShapeDtypeStruct((32, width), BF16),
            jax.ShapeDtypeStruct((3, shell_points.shape[1], 128), F32),
        ),
        in_specs=[pl.BlockSpec(memory_space=pltpu.HBM)] * 6,
        out_specs=(VMEM, VMEM, VMEM),
        scratch_shapes=[
            pltpu.VMEM(fibre_solve.shape, BF16),
            pltpu.VMEM(fibre_rhs.shape, BF16),
            pltpu.VMEM(fibre_points.shape, F32),
            pltpu.VMEM(density.shape, F32),
            pltpu.VMEM(shell_points.shape, F32),
            pltpu.SMEM((fibres,), jnp.int32),
            pltpu.SemaphoreType.DMA((fibres,)),
            pltpu.SemaphoreType.DMA((5,)),
        ],
        compiler_params=PARAMS,
        name="prepare",
    )(*[pltpu.with_memory_space_constraint(value, pltpu.HBM) for value in inputs])


def target_rows(place):
    sq = jnp.sum(place * place, axis=0, keepdims=True)
    high, middle, low = split3(place)
    one = jnp.ones_like(sq)
    zero = jnp.zeros_like(sq)
    sq_parts = split3(sq)
    return jnp.concatenate(
        [-2.0 * high, one] * 3
        + [-2.0 * middle, zero] * 2
        + [-2.0 * low, zero]
        + list(sq_parts)
        + [zero] * 5,
        axis=0,
    ).astype(BF16)


def source_rows(place):
    sq = jnp.sum(place * place, axis=0, keepdims=True) + smooth_sq
    high, middle, low = split3(jnp.concatenate([place, sq], axis=0))
    one = jnp.ones((3, place.shape[1]), F32)
    zero = jnp.zeros((5, place.shape[1]), F32)
    return jnp.concatenate([high, middle, low, high, middle, high, one, zero], axis=0).astype(BF16)


def source_terms(place, push, source):
    sq = jnp.sum(place * place, axis=0, keepdims=True) + 2.0 * smooth_sq
    rest = source - jnp.sum(place * push, axis=0, keepdims=True)
    terms = jnp.concatenate(
        [push, rest, sq * push - rest * place] + [place[a : a + 1] * push for a in range(3)], axis=0
    )
    return jnp.concatenate(split3(terms), axis=0).astype(BF16)


def sum_sources(target_ref, groups, block):
    totals = []
    for t in range(0, target_ref.shape[1], block):
        total = None
        for rows, terms in groups:
            width = rows.shape[1]
            lead = terms.shape[0] // 3
            step = min(block, width)
            for s in range(0, width, step):
                d = lax.dot_general(
                    rows[:, s : s + step],
                    target_ref[:, t : t + block],
                    (((0,), (0,)), ((), ())),
                    preferred_element_type=F32,
                )
                inverse = lax.rsqrt(d)
                cube = inverse * inverse * inverse
                high = cube.astype(BF16)
                low = (cube - high.astype(F32)).astype(BF16)
                term = terms[:, s : s + step]
                part = jnp.dot(term, high, preferred_element_type=F32)
                rest = jnp.dot(term[:lead], low, preferred_element_type=F32)
                part = jnp.concatenate([part[:lead] + rest, part[lead:]], axis=0)
                total = part if total is None else total + part
        totals.append(total[:lead] + total[lead : 2 * lead] + total[2 * lead :])
    return totals


def point_columns(points):
    count = points.shape[1]
    eye = lax.broadcasted_iota(jnp.int32, (count, count), 0) == lax.broadcasted_iota(
        jnp.int32, (count, count), 1
    )
    return [
        2.0 * jnp.sum(jnp.where(eye, points[c : c + 1], 0.0), axis=1, keepdims=True) - 1.0
        for c in range(3)
    ]


def direct(columns, place, push, source):
    offset = [columns[c] - place[c : c + 1] for c in range(3)]
    sq = offset[0] * offset[0] + offset[1] * offset[1] + offset[2] * offset[2]
    inverse = lax.rsqrt(sq + smooth_sq)
    cube = inverse * inverse * inverse
    along = source + (
        offset[0] * push[0:1] + offset[1] * push[1:2] + offset[2] * push[2:3]
    )
    spread = cube * (sq + 2.0 * smooth_sq)
    along = cube * along
    return [spread * push[c : c + 1] + along * offset[c] for c in range(3)]


def fold(value, lanes):
    total = value[:, :lanes]
    for at in range(lanes, value.shape[1], lanes):
        total = total + value[:, at : at + lanes]
    return total


def near_kernel(shifts, leaves, first, *refs):
    records_refs = refs[: len(shifts)]
    target_ref, column_ref = refs[len(shifts) : len(shifts) + 2]
    total_in, shell_in = (None, None) if first else refs[-4:-2]
    total_ref, shell_total_ref = refs[-2:]
    columns = [column_ref[c][:, 0:1] for c in range(3)]
    leaf = lax.axis_index("leaf")
    targets = target_ref.shape[1]
    block = min(256, targets)

    def run(chosen):
        groups = []
        shell = [None if first else shell_in[c] for c in range(3)]
        for at in chosen:
            for j in range(records_refs[at].shape[0]):
                record = records_refs[at].at[j]
                place = record[0, 0:3, :]
                if shifts[at] is not None:
                    axis = lax.broadcasted_iota(jnp.int32, place.shape, 0)
                    moved = (2 * shifts[at](leaf)).astype(F32)
                    place = place + jnp.where(axis == 0, moved, 0.0)
                push, source = record[1, 0:3, :], record[1, 3:4, :]
                groups.append((source_rows(place), source_terms(place, push, source)))
                for c, value in enumerate(direct(columns, place, push, source)):
                    value = fold(value, 128)
                    shell[c] = value if shell[c] is None else shell[c] + value
        for at, value in enumerate(sum_sources(target_ref, groups, block)):
            lanes = slice(at * block, (at + 1) * block)
            total_ref[:, lanes] = value if first else value + total_in[:, lanes]
        for c in range(3):
            shell_total_ref[c] = shell[c]

    def absent(shift):
        return shift is not None and any(not 0 <= i + shift(i) < leaves for i in range(leaves))

    everything = list(range(len(shifts)))
    always = [at for at in everything if not absent(shifts[at])]
    if always == everything:
        run(everything)
        return
    there = [leaf + shifts[at](leaf) for at in everything if at not in always]
    inside = functools.reduce(jnp.logical_and, [(x >= 0) & (x < leaves) for x in there])
    pl.when(inside)(lambda: run(everything))
    pl.when(jnp.logical_not(inside))(lambda: run(always))


def near(groups, own, totals):
    target_rows, columns = own
    targets = target_rows.shape[1]
    out = (jax.ShapeDtypeStruct((16, targets), F32), jax.ShapeDtypeStruct(columns.shape, F32))
    records, shifts = zip(*groups)
    size = sum(part.size for part in records)
    pairs = sum(part.shape[0] * part.shape[3] for part in records) * targets
    return pl.pallas_call(
        functools.partial(near_kernel, shifts, lax.axis_size("leaf"), totals is None),
        out_shape=out,
        in_specs=[VMEM] * (len(records) + (2 if totals is None else 4)),
        out_specs=(VMEM, VMEM),
        compiler_params=PARAMS,
        cost_estimate=pl.CostEstimate(
            flops=500 * pairs, bytes_accessed=size * 4, transcendentals=pairs
        ),
        name="near",
    )(*records, target_rows, columns, *(totals or ()))


def block_product(order, leaves, first, held_ref, block_ref):
    leaf, octant = lax.axis_index("leaf"), lax.axis_index("oct")
    octants = len(order)
    width = held_ref.shape[3]
    rows = block_ref.shape[2] // (leaves * octants * width)
    count = block_ref.shape[1]

    def body(at, sums):
        position = at + first
        seat = jnp.bitwise_xor(octant, position // 2 % 2)
        box = jnp.bitwise_xor(position, leaf)
        for j in range(octants):
            dens = held_ref[at // 2, (at % 2) * octants + j].astype(F32)
            owner = box * octants + jnp.bitwise_xor(seat, order[j])
            for r in range(rows):
                start = pl.multiple_of((owner * rows + r) * width, 128)
                sums = tuple(
                    sums[c] + block_ref[c, :, pl.ds(start, width)].astype(F32) * dens[r : r + 1]
                    for c in range(3)
                )
        return sums

    zero = jnp.zeros((count, width), F32)
    steps = 2 * held_ref.shape[0]
    return lax.fori_loop(0, steps, body, (zero, zero, zero), unroll=steps <= 4)


def shell_rows_kernel(order, leaves, held_ref, block_ref, product_ref):
    for c, value in enumerate(block_product(order, leaves, 0, held_ref, block_ref)):
        product_ref[c] = fold(value, 128)


def shell_rows(order, leaves, held, shell_block):
    return pl.pallas_call(
        functools.partial(shell_rows_kernel, order, leaves),
        out_shape=jax.ShapeDtypeStruct((3, shell_block.shape[1], 128), F32),
        in_specs=[VMEM] * 2,
        out_specs=VMEM,
        compiler_params=PARAMS,
        name="shell_rows",
    )(held, shell_block)


def finish_kernel(
    order,
    leaves,
    own_ref,
    target_ref,
    column_ref,
    held_ref,
    block_ref,
    product_in,
    total_in,
    shell_in,
    flow_ref,
    shell_flow_ref,
):
    leaf = lax.axis_index("leaf")
    octants = len(order)
    used = 2 * held_ref.shape[0] * octants
    boxes = -(-used // 128) * 128
    moments = []
    for c in range(4):
        parts = []
        for j in range(2 * held_ref.shape[0]):
            split = held_ref[j // 2, 2 * octants].astype(F32)
            at = ((j % 2) * 4 + c) * octants
            parts.append(jnp.sum(split[0:3, at : at + octants], axis=0, keepdims=True))
        if boxes > used:
            parts.append(jnp.zeros((1, boxes - used), F32))
        moments.append(jnp.concatenate(parts, axis=1))
    box = lax.broadcasted_iota(jnp.int32, (1, boxes), 1)
    away = jnp.bitwise_xor(box // 8 + 2, leaf) - leaf
    far = (jnp.abs(away) >= 2) & (box < used)
    away = jnp.where(far, away, 0)
    child = box % 8
    place = jnp.concatenate(
        [
            (2 * away + child % 2).astype(F32) - 0.5,
            (child // 2 % 2).astype(F32) - 0.5,
            (child // 4).astype(F32) - 0.5,
        ],
        axis=0,
    )
    push = jnp.where(far, jnp.concatenate(moments[0:3], axis=0), 0.0)
    source = jnp.where(far, moments[3], 0.0)
    x = own_ref[0, 0:3, :]
    groups = [(source_rows(place), source_terms(place, push, source))]
    far_sums = sum_sources(target_ref, groups, min(256, x.shape[1]))
    total = total_in[...] + jnp.concatenate(far_sums, axis=1)
    push_sum, rest_sum, constant = total[0:3], total[3:4], total[4:7]
    cross = [total[7 + 3 * a : 10 + 3 * a] for a in range(3)]
    flow = (
        jnp.sum(x * x, axis=0, keepdims=True) * push_sum
        + constant
        + x * (jnp.sum(x * push_sum, axis=0, keepdims=True) + rest_sum)
    )
    for a in range(3):
        flow = flow - 2.0 * x[a : a + 1] * cross[a]
    across = [
        jnp.sum(x * cross[c], axis=0, keepdims=True) for c in range(3)
    ]
    flow_ref[...] = stokes_scale * (flow - jnp.concatenate(across, axis=0))
    columns = [column_ref[c][:, 0:1] for c in range(3)]
    shell = [
        jnp.sum(shell_in[c] + fold(value, 128), axis=1, keepdims=True)
        for c, value in enumerate(direct(columns, place, push, source))
    ]
    count = block_ref.shape[1]
    product = [
        jnp.sum(product_in[c] + fold(value, 128), axis=1, keepdims=True)
        for c, value in enumerate(block_product(order, leaves, 2, held_ref, block_ref))
    ]
    eye = lax.broadcasted_iota(jnp.int32, (count, count), 0) == lax.broadcasted_iota(
        jnp.int32, (count, count), 1
    )
    for c in range(3):
        column = product[c] + stokes_scale * shell[c]
        shell_flow_ref[c : c + 1, :] = jnp.sum(jnp.where(eye, column, 0.0), axis=0, keepdims=True)


def finish(order, leaves, record, own, held, shell_block, product, totals):
    targets, points = record.shape[2], shell_block.shape[1]
    return pl.pallas_call(
        functools.partial(finish_kernel, order, leaves),
        out_shape=(
            jax.ShapeDtypeStruct((3, targets), F32),
            jax.ShapeDtypeStruct((3, points), F32),
        ),
        in_specs=[VMEM] * 8,
        out_specs=(VMEM, VMEM),
        compiler_params=PARAMS,
        name="finish",
    )(record, *own, held, shell_block, product, *totals)


def exchange(value, bits):
    devices = lax.axis_size("leaf") * lax.axis_size("oct")
    return lax.ppermute(value, ("leaf", "oct"), [(i, i ^ bits) for i in range(devices)])


def together(*values):
    return lax.optimization_barrier(values)


def shards(fibre_solve, fibre_rhs, fibre_points, fibre_owner, shell_points, shell_block, density):
    octants = lax.axis_size("oct")
    leaves = lax.axis_size("leaf")
    record, *own = prepare(
        fibre_solve, fibre_rhs, fibre_points, fibre_owner, density, shell_points
    )
    count, width = record.shape[1:]

    def inner_shift(leaf):
        return 1 - 2 * (leaf % 2)

    def outer_shift(leaf):
        return 2 * (leaf % 2) - 1

    order = [0]
    for bit in [1 << b for b in range(1, octants.bit_length() - 1)]:
        order = order + [j ^ bit ^ 1 for j in order]
    arrived = [exchange(record, j) for j in order[:0:-1]][::-1]
    totals = near([(record[None], None)], own, None)
    *arrived, totals = together(*arrived[::-1], totals)
    arrived = arrived[::-1]
    fresh = jnp.stack(arrived)
    records = jnp.stack([record] + arrived)
    swaps = []
    for leaf in range(leaves):
        there = leaf + outer_shift(leaf)
        there = there if 0 <= there < leaves else leaf
        swaps += [(leaf * octants + o, there * octants + (o ^ 1)) for o in range(octants)]
    order = order + [j ^ 1 for j in order]
    inner = exchange(records, octants + 1)
    outer = lax.ppermute(records[:, :2], ("leaf", "oct"), swaps)
    late = exchange(records, 1)
    late, totals = together(late, totals)
    records = jnp.concatenate([records, late], axis=0)
    totals = near([(fresh, None), (late, None)], own, totals)
    outer, inner, totals = together(outer, inner, totals)
    late_inner, late_outer = exchange(inner, 1), exchange(outer, 1)
    totals = near([(inner, inner_shift)], own, totals)
    late_inner, late_outer, totals = together(late_inner, late_outer, totals)
    outer = jnp.concatenate([outer, late_outer], axis=0)
    inner = jnp.concatenate([late_inner, inner], axis=0)
    dens = jnp.concatenate([records[:, 2], inner[:, 2]], axis=0).astype(BF16)
    moments = jnp.concatenate(
        [jnp.sum(part[:, 0, 3, : 4 * octants], axis=0)[None] for part in (records, inner)], axis=1
    )
    high = lax.reduce_precision(moments, 8, 7)
    middle = lax.reduce_precision(moments - high, 8, 7)
    low = lax.reduce_precision(moments - high - middle, 8, 7)
    parts = jnp.concatenate([high, middle, low], axis=0).astype(BF16)
    parts = jnp.pad(parts, ((0, count - 3), (0, width - parts.shape[1])))
    held = jnp.concatenate([dens, parts[None]], axis=0)[None]
    bits = [(1 << b) * octants for b in range(1, leaves.bit_length() - 1)]
    rest = exchange(held, bits[0] + 1)
    product = shell_rows(tuple(order), leaves, held, shell_block)
    product, totals = together(product, totals)
    totals = near([(late_inner, inner_shift), (outer, outer_shift)], own, totals)
    for bit in bits[1:]:
        whole = jnp.concatenate([held, rest], axis=0)
        rest = jnp.concatenate([rest, exchange(whole, bit)], axis=0)
    return finish(tuple(order), leaves, record, own, rest, shell_block, product, totals)


def solution(mesh):
    placed = (
        P(("leaf", "oct"), None, None),
        P(("leaf", "oct"), None),
        P(("leaf", "oct"), None),
        P(("leaf", "oct"), None),
        P(None, ("leaf", "oct")),
        P(None, ("leaf", "oct"), None),
        P(("leaf", "oct")),
    )
    return jax.shard_map(
        shards,
        mesh=mesh,
        in_specs=placed,
        out_specs=(P(None, ("leaf", "oct")), P(None, ("leaf", "oct"))),
        check_vma=False,
    )
```

```python
import functools
import math

import jax
import jax.numpy as jnp
from jax import lax
from jax.experimental import pallas as pl
from jax.experimental.pallas import tpu as pltpu
from jax.sharding import PartitionSpec as P

smooth_sq = 0.01
stokes_scale = 1.0 / (8.0 * math.pi)
F32 = jnp.float32
BF16 = jnp.bfloat16
VMEM = pl.BlockSpec(memory_space=pltpu.VMEM)
PARAMS = pltpu.CompilerParams(vmem_limit_bytes=40 * 2**20)


def split3(value):
    high = value.astype(BF16).astype(F32)
    rest = value - high
    middle = rest.astype(BF16).astype(F32)
    return high, middle, (rest - middle).astype(BF16).astype(F32)


def prepare_kernel(*refs):
    solve_hbm, rhs_hbm, points_hbm, owner_hbm, density_hbm, shell_hbm = refs[:6]
    record_ref, target_ref, column_ref = refs[6:9]
    solve_ref, rhs_ref, points_ref, density_ref, shell_ref, owner_ref, solve_sem, sem = refs[9:]
    fibres, quads = rhs_ref.shape
    nodes = quads // 4
    width = record_ref.shape[2]
    part = math.gcd(fibres, 4)
    copies = [
        pltpu.make_async_copy(owner_hbm, owner_ref, sem.at[0]),
        pltpu.make_async_copy(points_hbm, points_ref, sem.at[1]),
        pltpu.make_async_copy(rhs_hbm, rhs_ref, sem.at[2]),
        pltpu.make_async_copy(density_hbm, density_ref, sem.at[3]),
        pltpu.make_async_copy(shell_hbm, shell_ref, sem.at[4]),
    ]
    solves = [
        pltpu.make_async_copy(
            solve_hbm.at[pl.ds(f, part)], solve_ref.at[pl.ds(f, part)], solve_sem.at[f // part]
        )
        for f in range(0, fibres, part)
    ]
    for copy in copies + solves:
        copy.start()
    for copy in copies:
        copy.wait()
    record_ref[2] = jnp.zeros(record_ref.shape[1:], F32)
    for r in range(density_ref.shape[0] // width):
        dens = density_ref[r * width : (r + 1) * width].reshape(1, width)
        record_ref[2, r : r + 1, :] = dens.astype(BF16).astype(F32)
    row = lax.broadcasted_iota(jnp.int32, (fibres, 1), 0)
    owner = jnp.zeros((fibres, 1), jnp.int32)
    for f in range(fibres):
        owner = jnp.where(row == f, owner_ref[f], owner)
    points = points_ref[...]
    corner = [owner % 2, owner // 2 % 2, owner // 4]
    place = [
        points[:, c * nodes : (c + 1) * nodes] + (corner[c].astype(F32) - 1.0) for c in range(3)
    ]
    for f in range(fibres):
        lanes = slice(f * nodes, (f + 1) * nodes)
        for c in range(3):
            record_ref[0, c : c + 1, lanes] = place[c][f : f + 1, :]
    quad_weight = points[:, 3 * nodes :]
    rhs = rhs_ref[...]
    forces = jnp.zeros((fibres, quads), F32)
    for f in range(fibres):
        if f % part == 0:
            solves[f // part].wait()
        product = lax.dot_general(
            rhs, solve_ref[f], (((1,), (1,)), ((), ())), preferred_element_type=F32
        )
        forces = jnp.where(row == f, product, forces)
    pushes = forces * jnp.concatenate([quad_weight] * 4, axis=1)
    for f in range(fibres):
        lanes = slice(f * nodes, (f + 1) * nodes)
        for c in range(4):
            record_ref[1, c : c + 1, lanes] = pushes[f : f + 1, c * nodes : (c + 1) * nodes]
    lane = lax.broadcasted_iota(jnp.int32, (fibres, width), 1)
    sums = jnp.zeros((fibres, width), F32)
    for c in range(4):
        box_sum = jnp.sum(pushes[:, c * nodes : (c + 1) * nodes], axis=1, keepdims=True)
        sums = jnp.where(lane == owner + 8 * c, box_sum, sums)
    record_ref[0, 3:4, :] = jnp.sum(sums, axis=0, keepdims=True)
    target_ref[...] = target_rows(record_ref[0, 0:3, :])
    for c, column in enumerate(point_columns(shell_ref[...])):
        column_ref[c] = jnp.broadcast_to(column, column_ref.shape[1:])


def prepare(fibre_solve, fibre_rhs, fibre_points, fibre_owner, density, shell_points):
    fibres, quads = fibre_points.shape
    width = fibres * quads // 4
    inputs = (
        fibre_solve,
        fibre_rhs,
        fibre_points,
        fibre_owner.reshape(fibres),
        density,
        shell_points,
    )
    return pl.pallas_call(
        prepare_kernel,
        out_shape=(
            jax.ShapeDtypeStruct((3, 4, width), F32),
            jax.ShapeDtypeStruct((32, width), BF16),
            jax.ShapeDtypeStruct((3, shell_points.shape[1], 128), F32),
        ),
        in_specs=[pl.BlockSpec(memory_space=pltpu.HBM)] * 6,
        out_specs=(VMEM, VMEM, VMEM),
        scratch_shapes=[
            pltpu.VMEM(fibre_solve.shape, BF16),
            pltpu.VMEM(fibre_rhs.shape, BF16),
            pltpu.VMEM(fibre_points.shape, F32),
            pltpu.VMEM(density.shape, F32),
            pltpu.VMEM(shell_points.shape, F32),
            pltpu.SMEM((fibres,), jnp.int32),
            pltpu.SemaphoreType.DMA((fibres,)),
            pltpu.SemaphoreType.DMA((5,)),
        ],
        compiler_params=PARAMS,
        name="prepare",
    )(*[pltpu.with_memory_space_constraint(value, pltpu.HBM) for value in inputs])


def target_rows(place):
    sq = jnp.sum(place * place, axis=0, keepdims=True)
    high, middle, low = split3(place)
    one = jnp.ones_like(sq)
    zero = jnp.zeros_like(sq)
    sq_parts = split3(sq)
    return jnp.concatenate(
        [-2.0 * high, one] * 3
        + [-2.0 * middle, zero] * 2
        + [-2.0 * low, zero]
        + list(sq_parts)
        + [zero] * 5,
        axis=0,
    ).astype(BF16)


def source_rows(place):
    sq = jnp.sum(place * place, axis=0, keepdims=True) + smooth_sq
    high, middle, low = split3(jnp.concatenate([place, sq], axis=0))
    one = jnp.ones((3, place.shape[1]), F32)
    zero = jnp.zeros((5, place.shape[1]), F32)
    return jnp.concatenate([high, middle, low, high, middle, high, one, zero], axis=0).astype(BF16)


def source_terms(place, push, source):
    sq = jnp.sum(place * place, axis=0, keepdims=True) + 2.0 * smooth_sq
    rest = source - jnp.sum(place * push, axis=0, keepdims=True)
    terms = jnp.concatenate(
        [push, rest, sq * push - rest * place] + [place[a : a + 1] * push for a in range(3)], axis=0
    )
    return jnp.concatenate(split3(terms), axis=0).astype(BF16)


def sum_sources(target_ref, groups, block):
    totals = []
    for t in range(0, target_ref.shape[1], block):
        total = None
        for rows, terms in groups:
            width = rows.shape[1]
            lead = terms.shape[0] // 3
            step = min(block, width)
            for s in range(0, width, step):
                d = lax.dot_general(
                    rows[:, s : s + step],
                    target_ref[:, t : t + block],
                    (((0,), (0,)), ((), ())),
                    preferred_element_type=F32,
                )
                inverse = lax.rsqrt(d)
                cube = inverse * inverse * inverse
                high = cube.astype(BF16)
                low = (cube - high.astype(F32)).astype(BF16)
                term = terms[:, s : s + step]
                part = jnp.dot(term, high, preferred_element_type=F32)
                rest = jnp.dot(term[:lead], low, preferred_element_type=F32)
                part = jnp.concatenate([part[:lead] + rest, part[lead:]], axis=0)
                total = part if total is None else total + part
        totals.append(total[:lead] + total[lead : 2 * lead] + total[2 * lead :])
    return totals


def point_columns(points):
    count = points.shape[1]
    eye = lax.broadcasted_iota(jnp.int32, (count, count), 0) == lax.broadcasted_iota(
        jnp.int32, (count, count), 1
    )
    return [
        2.0 * jnp.sum(jnp.where(eye, points[c : c + 1], 0.0), axis=1, keepdims=True) - 1.0
        for c in range(3)
    ]


def direct(columns, place, push, source):
    offset = [columns[c] - place[c : c + 1] for c in range(3)]
    sq = offset[0] * offset[0] + offset[1] * offset[1] + offset[2] * offset[2]
    inverse = lax.rsqrt(sq + smooth_sq)
    cube = inverse * inverse * inverse
    along = source + (
        offset[0] * push[0:1] + offset[1] * push[1:2] + offset[2] * push[2:3]
    )
    spread = cube * (sq + 2.0 * smooth_sq)
    along = cube * along
    return [spread * push[c : c + 1] + along * offset[c] for c in range(3)]


def fold(value, lanes):
    total = value[:, :lanes]
    for at in range(lanes, value.shape[1], lanes):
        total = total + value[:, at : at + lanes]
    return total


def near_kernel(shifts, leaves, first, *refs):
    records_refs = refs[: len(shifts)]
    target_ref, column_ref = refs[len(shifts) : len(shifts) + 2]
    total_in, shell_in = (None, None) if first else refs[-4:-2]
    total_ref, shell_total_ref = refs[-2:]
    columns = [column_ref[c][:, 0:1] for c in range(3)]
    leaf = lax.axis_index("leaf")
    targets = target_ref.shape[1]
    block = min(256, targets)

    def run(chosen):
        groups = []
        shell = [None if first else shell_in[c] for c in range(3)]
        for at in chosen:
            for j in range(records_refs[at].shape[0]):
                record = records_refs[at].at[j]
                place = record[0, 0:3, :]
                if shifts[at] is not None:
                    axis = lax.broadcasted_iota(jnp.int32, place.shape, 0)
                    moved = (2 * shifts[at](leaf)).astype(F32)
                    place = place + jnp.where(axis == 0, moved, 0.0)
                push, source = record[1, 0:3, :], record[1, 3:4, :]
                groups.append((source_rows(place), source_terms(place, push, source)))
                for c, value in enumerate(direct(columns, place, push, source)):
                    value = fold(value, 128)
                    shell[c] = value if shell[c] is None else shell[c] + value
        for at, value in enumerate(sum_sources(target_ref, groups, block)):
            lanes = slice(at * block, (at + 1) * block)
            total_ref[:, lanes] = value if first else value + total_in[:, lanes]
        for c in range(3):
            shell_total_ref[c] = shell[c]

    def absent(shift):
        return shift is not None and any(not 0 <= i + shift(i) < leaves for i in range(leaves))

    everything = list(range(len(shifts)))
    always = [at for at in everything if not absent(shifts[at])]
    if always == everything:
        run(everything)
        return
    there = [leaf + shifts[at](leaf) for at in everything if at not in always]
    inside = functools.reduce(jnp.logical_and, [(x >= 0) & (x < leaves) for x in there])
    pl.when(inside)(lambda: run(everything))
    pl.when(jnp.logical_not(inside))(lambda: run(always))


def near(groups, own, totals):
    target_rows, columns = own
    targets = target_rows.shape[1]
    out = (jax.ShapeDtypeStruct((16, targets), F32), jax.ShapeDtypeStruct(columns.shape, F32))
    records, shifts = zip(*groups)
    size = sum(part.size for part in records)
    pairs = sum(part.shape[0] * part.shape[3] for part in records) * targets
    return pl.pallas_call(
        functools.partial(near_kernel, shifts, lax.axis_size("leaf"), totals is None),
        out_shape=out,
        in_specs=[VMEM] * (len(records) + (2 if totals is None else 4)),
        out_specs=(VMEM, VMEM),
        compiler_params=PARAMS,
        cost_estimate=pl.CostEstimate(
            flops=500 * pairs, bytes_accessed=size * 4, transcendentals=pairs
        ),
        name="near",
    )(*records, target_rows, columns, *(totals or ()))


def block_product(order, leaves, first, held_ref, block_ref):
    leaf, octant = lax.axis_index("leaf"), lax.axis_index("oct")
    octants = len(order)
    width = held_ref.shape[3]
    rows = block_ref.shape[2] // (leaves * octants * width)
    count = block_ref.shape[1]

    def body(at, sums):
        position = at + first
        seat = jnp.bitwise_xor(octant, position // 2 % 2)
        box = jnp.bitwise_xor(position, leaf)
        for j in range(octants):
            dens = held_ref[at // 2, (at % 2) * octants + j].astype(F32)
            owner = box * octants + jnp.bitwise_xor(seat, order[j])
            for r in range(rows):
                start = pl.multiple_of((owner * rows + r) * width, 128)
                sums = tuple(
                    sums[c] + block_ref[c, :, pl.ds(start, width)].astype(F32) * dens[r : r + 1]
                    for c in range(3)
                )
        return sums

    zero = jnp.zeros((count, width), F32)
    steps = 2 * held_ref.shape[0]
    return lax.fori_loop(0, steps, body, (zero, zero, zero), unroll=steps <= 4)


def shell_rows_kernel(order, leaves, held_ref, block_ref, product_ref):
    for c, value in enumerate(block_product(order, leaves, 0, held_ref, block_ref)):
        product_ref[c] = fold(value, 128)


def shell_rows(order, leaves, held, shell_block):
    return pl.pallas_call(
        functools.partial(shell_rows_kernel, order, leaves),
        out_shape=jax.ShapeDtypeStruct((3, shell_block.shape[1], 128), F32),
        in_specs=[VMEM] * 2,
        out_specs=VMEM,
        compiler_params=PARAMS,
        name="shell_rows",
    )(held, shell_block)


def finish_kernel(
    order,
    leaves,
    own_ref,
    target_ref,
    column_ref,
    held_ref,
    block_ref,
    product_in,
    total_in,
    shell_in,
    flow_ref,
    shell_flow_ref,
):
    leaf = lax.axis_index("leaf")
    octants = len(order)
    used = 2 * held_ref.shape[0] * octants
    boxes = -(-used // 128) * 128
    moments = []
    for c in range(4):
        parts = []
        for j in range(2 * held_ref.shape[0]):
            split = held_ref[j // 2, 2 * octants].astype(F32)
            at = ((j % 2) * 4 + c) * octants
            parts.append(jnp.sum(split[0:3, at : at + octants], axis=0, keepdims=True))
        if boxes > used:
            parts.append(jnp.zeros((1, boxes - used), F32))
        moments.append(jnp.concatenate(parts, axis=1))
    box = lax.broadcasted_iota(jnp.int32, (1, boxes), 1)
    away = jnp.bitwise_xor(box // 8 + 2, leaf) - leaf
    far = (jnp.abs(away) >= 2) & (box < used)
    away = jnp.where(far, away, 0)
    child = box % 8
    place = jnp.concatenate(
        [
            (2 * away + child % 2).astype(F32) - 0.5,
            (child // 2 % 2).astype(F32) - 0.5,
            (child // 4).astype(F32) - 0.5,
        ],
        axis=0,
    )
    push = jnp.where(far, jnp.concatenate(moments[0:3], axis=0), 0.0)
    source = jnp.where(far, moments[3], 0.0)
    x = own_ref[0, 0:3, :]
    groups = [(source_rows(place), source_terms(place, push, source))]
    far_sums = sum_sources(target_ref, groups, min(256, x.shape[1]))
    total = total_in[...] + jnp.concatenate(far_sums, axis=1)
    push_sum, rest_sum, constant = total[0:3], total[3:4], total[4:7]
    cross = [total[7 + 3 * a : 10 + 3 * a] for a in range(3)]
    flow = (
        jnp.sum(x * x, axis=0, keepdims=True) * push_sum
        + constant
        + x * (jnp.sum(x * push_sum, axis=0, keepdims=True) + rest_sum)
    )
    for a in range(3):
        flow = flow - 2.0 * x[a : a + 1] * cross[a]
    across = [
        jnp.sum(x * cross[c], axis=0, keepdims=True) for c in range(3)
    ]
    flow_ref[...] = stokes_scale * (flow - jnp.concatenate(across, axis=0))
    columns = [column_ref[c][:, 0:1] for c in range(3)]
    shell = [
        jnp.sum(shell_in[c] + fold(value, 128), axis=1, keepdims=True)
        for c, value in enumerate(direct(columns, place, push, source))
    ]
    count = block_ref.shape[1]
    product = [
        jnp.sum(product_in[c] + fold(value, 128), axis=1, keepdims=True)
        for c, value in enumerate(block_product(order, leaves, 2, held_ref, block_ref))
    ]
    eye = lax.broadcasted_iota(jnp.int32, (count, count), 0) == lax.broadcasted_iota(
        jnp.int32, (count, count), 1
    )
    for c in range(3):
        column = product[c] + stokes_scale * shell[c]
        shell_flow_ref[c : c + 1, :] = jnp.sum(jnp.where(eye, column, 0.0), axis=0, keepdims=True)


def finish(order, leaves, record, own, held, shell_block, product, totals):
    targets, points = record.shape[2], shell_block.shape[1]
    return pl.pallas_call(
        functools.partial(finish_kernel, order, leaves),
        out_shape=(
            jax.ShapeDtypeStruct((3, targets), F32),
            jax.ShapeDtypeStruct((3, points), F32),
        ),
        in_specs=[VMEM] * 8,
        out_specs=(VMEM, VMEM),
        compiler_params=PARAMS,
        name="finish",
    )(record, *own, held, shell_block, product, *totals)


def exchange(value, bits):
    devices = lax.axis_size("leaf") * lax.axis_size("oct")
    return lax.ppermute(value, ("leaf", "oct"), [(i, i ^ bits) for i in range(devices)])


def together(*values):
    return lax.optimization_barrier(values)


def shards(fibre_solve, fibre_rhs, fibre_points, fibre_owner, shell_points, shell_block, density):
    octants = lax.axis_size("oct")
    leaves = lax.axis_size("leaf")
    record, *own = prepare(
        fibre_solve, fibre_rhs, fibre_points, fibre_owner, density, shell_points
    )
    count, width = record.shape[1:]

    def inner_shift(leaf):
        return 1 - 2 * (leaf % 2)

    def outer_shift(leaf):
        return 2 * (leaf % 2) - 1

    order = [0]
    for bit in [1 << b for b in range(1, octants.bit_length() - 1)]:
        order = order + [j ^ bit ^ 1 for j in order]
    arrived = [exchange(record, order[1 + i]) for i in (1, 2, 0)]
    totals = near([(record[None], None)], own, None)
    *arrived, totals = together(*arrived, totals)
    arrived = [arrived[i] for i in [2, 0, 1]]
    fresh = jnp.stack(arrived)
    records = jnp.stack([record] + arrived)
    swaps = []
    for leaf in range(leaves):
        there = leaf + outer_shift(leaf)
        there = there if 0 <= there < leaves else leaf
        swaps += [(leaf * octants + o, there * octants + (o ^ 1)) for o in range(octants)]
    order = order + [j ^ 1 for j in order]
    inner = exchange(records, octants + 1)
    outer = lax.ppermute(records[:, :2], ("leaf", "oct"), swaps)
    late = exchange(records, 1)
    late, totals = together(late, totals)
    records = jnp.concatenate([records, late], axis=0)
    totals = near([(fresh, None), (late, None)], own, totals)
    outer, inner, totals = together(outer, inner, totals)
    late_inner, late_outer = exchange(inner, 1), exchange(outer, 1)
    totals = near([(inner, inner_shift)], own, totals)
    late_inner, late_outer, totals = together(late_inner, late_outer, totals)
    outer = jnp.concatenate([outer, late_outer], axis=0)
    inner = jnp.concatenate([late_inner, inner], axis=0)
    dens = jnp.concatenate([records[:, 2], inner[:, 2]], axis=0).astype(BF16)
    moments = jnp.concatenate(
        [jnp.sum(part[:, 0, 3, : 4 * octants], axis=0)[None] for part in (records, inner)], axis=1
    )
    high = lax.reduce_precision(moments, 8, 7)
    middle = lax.reduce_precision(moments - high, 8, 7)
    low = lax.reduce_precision(moments - high - middle, 8, 7)
    parts = jnp.concatenate([high, middle, low], axis=0).astype(BF16)
    parts = jnp.pad(parts, ((0, count - 3), (0, width - parts.shape[1])))
    held = jnp.concatenate([dens, parts[None]], axis=0)[None]
    bits = [(1 << b) * octants for b in range(1, leaves.bit_length() - 1)]
    rest = exchange(held, bits[0] + 1)
    product = shell_rows(tuple(order), leaves, held, shell_block)
    product, totals = together(product, totals)
    totals = near([(late_inner, inner_shift), (outer, outer_shift)], own, totals)
    for bit in bits[1:]:
        whole = jnp.concatenate([held, rest], axis=0)
        rest = jnp.concatenate([rest, exchange(whole, bit)], axis=0)
    return finish(tuple(order), leaves, record, own, rest, shell_block, product, totals)


def solution(mesh):
    placed = (
        P(("leaf", "oct"), None, None),
        P(("leaf", "oct"), None),
        P(("leaf", "oct"), None),
        P(("leaf", "oct"), None),
        P(None, ("leaf", "oct")),
        P(None, ("leaf", "oct"), None),
        P(("leaf", "oct")),
    )
    return jax.shard_map(
        shards,
        mesh=mesh,
        in_specs=placed,
        out_specs=(P(None, ("leaf", "oct")), P(None, ("leaf", "oct"))),
        check_vma=False,
    )
```
